256 devices in a mesh: section: 32 (over z_lo, x, core), rep: 8 (over z_hi, y).
Axes of the slice: x: 4, y: 4, z: 8 (z_hi: 2, z_lo: 4; z = z_hi * 4 + z_lo), core: 2. Of those that a mesh axis runs over, the one named last changes fastest.
Arguments:
- features: bfloat16 [16384, 256], P('section'), may hold values from -6 to 6
- cotangent: bfloat16 [16384, 256], P('section'), may hold values from -6 to 6
- degrees: int32 [16384], P('section'), may hold values from 4 to 64
- blocks: bfloat16 [32, 8, 48, 128, 128], P('section', 'rep'), may hold values from -4 to 4
- block_rows: int32 [32, 8, 48], P('section', 'rep'), may hold values from 0 to 3
- block_cols: int32 [32, 8, 48], P('section', 'rep'), may hold values from 0 to 15
- block_count: int32 [32, 8], P('section', 'rep'), may hold values from 1 to 48, as said below
- w_self: bfloat16 [256, 256], replicated, may hold values from -0.375 to 0.375
- w_neigh: bfloat16 [256, 256], replicated, may hold values from -0.375 to 0.375
Outputs:
- activated: bfloat16 [16384, 256], P('section')
- feature_grad: float32 [16384, 256], P('section')
- grad_self: float32 [256, 256], replicated
- grad_neigh: float32 [256, 256], replicated
The draws below stay inside these ranges and needn't reach their ends.
Inputs may be any that keep to these rules, and one draw needn't show every extreme that they name: `block_count`: live slots come first in each device's list; some device has all 48 slots live.
All inputs are finite; a program needn't handle non-finite values.
Results may differ from the reference program's by a relative error of at most 0.025.
Values may be sent and summed in bfloat16 or wider, within the bound.
No kernel may reach another device: no remote copies, remote signals or barrier semaphores. Data moves between devices by JAX's collectives and lax.ppermute only.
A program may use at most 64 MiB of HBM per device.

```python
import jax
import jax.numpy as jnp
from jax import lax

WIDTH = 256
BLOCK = 128
ROWS = 512
SLOTS = 48
NODES = 16384
N_SECTION = 32
N_REP = 8


def draw_block_count(key, part):
    key = jax.random.fold_in(key, 7)
    key_counts, key_full = jax.random.split(key)
    raw_values = jax.random.randint(key_counts, (N_SECTION * N_REP,), 1, SLOTS + 1)
    counts = jnp.maximum(raw_values * raw_values // SLOTS, 1)
    chosen = jax.random.randint(key_full, (), 0, N_SECTION * N_REP)
    counts = jnp.where(jnp.arange(N_SECTION * N_REP) == chosen, SLOTS, counts)
    return counts.reshape(N_SECTION, N_REP).astype(jnp.int32)


def with_ends(entries, rng, low, largest):
    spot = [jax.random.randint(jax.random.fold_in(rng, axis), (), 0, length) for axis, length in enumerate(entries.shape)]
    main_axis = entries.shape.index(max(entries.shape))
    beside = spot[:main_axis] + [(spot[main_axis] + 1) % entries.shape[main_axis]] + spot[main_axis + 1:]
    return entries.at[tuple(spot)].set(low).at[tuple(beside)].set(largest)


def shard_levels(key, dims, cuts, least, top_value):
    level = 1.0
    for dim, parts in cuts:
        draws = jax.random.uniform(jax.random.fold_in(jax.random.fold_in(key, 6), dim), (parts,), jnp.float32, least / len(cuts), top_value / len(cuts))
        level = level * jnp.repeat(jnp.exp(draws), dims[dim] // parts).reshape((-1,) + (1,) * (len(dims) - 1 - dim))
    return level


def bell_draw(stream_key, dims, deviation, most, cuts=(), kind=jnp.bfloat16):
    drawn = deviation * jax.random.normal(stream_key, dims, jnp.float32)
    if cuts:
        drawn = drawn * shard_levels(stream_key, dims, cuts, -0.22, 0.18)
    return jnp.clip(drawn, -most, most).astype(kind)


def setup_inputs(seed: int = 0) -> dict:
    keys = jax.random.split(jax.random.key(seed), 10)
    features = bell_draw(keys[0], (NODES, WIDTH), 1.0, 6.0, ((0, 32),))
    cotangent = bell_draw(keys[1], (NODES, WIDTH), 1.0, 6.0, ((0, 32),))
    degrees = with_ends(jax.random.randint(keys[2], (NODES,), 4, 65), jax.random.fold_in(keys[2], 1), 4, 64).astype(jnp.int32)
    blocks = bell_draw(keys[3], (N_SECTION, N_REP, SLOTS, BLOCK, BLOCK), 0.3, 4.0, ((0, 32), (1, 8)))
    block_rows = with_ends(jax.random.randint(keys[4], (N_SECTION, N_REP, SLOTS), 0, ROWS // BLOCK), jax.random.fold_in(keys[4], 1), 0, (ROWS // BLOCK) - 1).astype(jnp.int32)
    block_cols = with_ends(jax.random.randint(keys[5], (N_SECTION, N_REP, SLOTS), 0, N_SECTION // N_REP * (ROWS // BLOCK)), jax.random.fold_in(keys[5], 1), 0, (N_SECTION // N_REP * (ROWS // BLOCK)) - 1).astype(jnp.int32)
    block_count = draw_block_count(jax.random.fold_in(keys[9], 71), 0)
    w_self = bell_draw(keys[7], (WIDTH, WIDTH), WIDTH ** -0.5, 0.375)
    w_neigh = bell_draw(keys[8], (WIDTH, WIDTH), WIDTH ** -0.5, 0.375)
    return dict(features=features, cotangent=cotangent, degrees=degrees, blocks=blocks, block_rows=block_rows, block_cols=block_cols, block_count=block_count, w_self=w_self, w_neigh=w_neigh)


def reference(features, cotangent, degrees, blocks, block_rows, block_cols, block_count, w_self, w_neigh):
    panel_count = N_SECTION // N_REP
    row_blocks = ROWS // BLOCK
    device_total = N_SECTION * N_REP
    flat_tiles = blocks.reshape(device_total, SLOTS, BLOCK, BLOCK)
    flat_rows = block_rows.reshape(device_total, SLOTS)
    flat_cols = block_cols.reshape(device_total, SLOTS)
    flat_count = block_count.reshape(device_total)
    grouped = features.reshape(panel_count, N_REP, ROWS, WIDTH)
    slot_index = jnp.arange(SLOTS, dtype=jnp.int32)

    def forward_device(device):
        replica = device % N_REP
        columns = lax.dynamic_index_in_dim(grouped, replica, 1, keepdims=False)
        columns = columns.reshape(panel_count * row_blocks, BLOCK, WIDTH)
        picked = columns[flat_cols[device]]
        live_mask = (slot_index < flat_count[device]).astype(jnp.float32)
        products = jnp.einsum("bij,bjf->bif", flat_tiles[device].astype(jnp.float32), picked.astype(jnp.float32))
        products = products * live_mask[:, None, None]
        summed_rows = jax.ops.segment_sum(products, flat_rows[device], num_segments=row_blocks)
        return summed_rows.reshape(ROWS, WIDTH)

    partials = lax.map(forward_device, jnp.arange(device_total, dtype=jnp.int32))
    summed = jnp.sum(partials.reshape(N_SECTION, N_REP, ROWS, WIDTH), axis=1).reshape(NODES, WIDTH)
    degree_value = degrees.astype(jnp.float32)
    mean_input = (summed / degree_value[:, None]).astype(jnp.bfloat16)
    preact = jnp.dot(features, w_self, preferred_element_type=jnp.float32) + jnp.dot(mean_input, w_neigh, preferred_element_type=jnp.float32)
    sigmoid_value = jax.nn.sigmoid(preact)
    activated = (preact * sigmoid_value).astype(jnp.bfloat16)
    slope_value = sigmoid_value * (1.0 + preact * (1.0 - sigmoid_value))
    pre_grad = (cotangent.astype(jnp.float32) * slope_value).astype(jnp.bfloat16)
    grad_self = jnp.dot(features.T, pre_grad, preferred_element_type=jnp.float32)
    grad_neigh = jnp.dot(mean_input.T, pre_grad, preferred_element_type=jnp.float32)
    down_grad = (jnp.dot(pre_grad, w_neigh.T, preferred_element_type=jnp.float32) / degree_value[:, None]).astype(jnp.bfloat16)
    self_part = jnp.dot(pre_grad, w_self.T, preferred_element_type=jnp.float32)
    down_panels = down_grad.reshape(N_SECTION, row_blocks, BLOCK, WIDTH)

    def backward_step(total, device):
        section_position = device // N_REP
        replica = device % N_REP
        own_rows = lax.dynamic_index_in_dim(down_panels, section_position, 0, keepdims=False)
        by_rows = own_rows[flat_rows[device]]
        live_mask = (slot_index < flat_count[device]).astype(jnp.float32)
        back_terms = jnp.einsum("bji,bjf->bif", flat_tiles[device].astype(jnp.float32), by_rows.astype(jnp.float32))
        back_terms = back_terms * live_mask[:, None, None]
        column_sums = jax.ops.segment_sum(back_terms, flat_cols[device], num_segments=panel_count * row_blocks)
        column_sums = column_sums.reshape(panel_count, ROWS, WIDTH)
        return total.at[:, replica].add(column_sums), None

    start_total = jnp.zeros((panel_count, N_REP, ROWS, WIDTH), jnp.float32)
    transposed, unused_out = lax.scan(backward_step, start_total, jnp.arange(device_total, dtype=jnp.int32))
    feature_grad = self_part + transposed.reshape(NODES, WIDTH)
    return (activated, feature_grad, grad_self, grad_neigh)
```

```python
import jax
import jax.numpy as jnp
from jax import lax
from jax.experimental import pallas as pl
from jax.experimental.pallas import tpu as pltpu
from jax.sharding import PartitionSpec as P

BLOCK = 128
F32 = jnp.float32
BF16 = jnp.bfloat16


def densify_kernel(rows_ref, cols_ref, scalars_ref, blocks_ref, dense_ref, flipped_ref, total):
    total[...] = jnp.zeros_like(total)
    live = scalars_ref[0]
    core = scalars_ref[1]

    def add_slot(slot, carry):
        row = rows_ref[slot]
        col = cols_ref[slot]
        panel = col // 4
        within = col % 4
        half = (within // 2 + core) % 2
        place = half * 8 + panel * 2 + within % 2
        total[row, place] += blocks_ref[slot].astype(F32)
        return carry

    lax.fori_loop(0, live, add_slot, 0)
    for i in range(4):
        for j in range(16):
            tile = total[i, j]
            dense_ref[i * BLOCK : (i + 1) * BLOCK, j * BLOCK : (j + 1) * BLOCK] = tile.astype(BF16)
            flipped_ref[j * BLOCK : (j + 1) * BLOCK, i * BLOCK : (i + 1) * BLOCK] = tile.T.astype(
                BF16
            )


def densify(tiles, rows, cols, scalars):
    smem = pl.BlockSpec(memory_space=pltpu.SMEM)
    vmem = pl.BlockSpec(memory_space=pltpu.VMEM)
    return pl.pallas_call(
        densify_kernel,
        out_shape=(
            jax.ShapeDtypeStruct((512, 2048), BF16),
            jax.ShapeDtypeStruct((2048, 512), BF16),
        ),
        in_specs=[smem, smem, smem, vmem],
        out_specs=(vmem, vmem),
        scratch_shapes=[pltpu.VMEM((4, 16, BLOCK, BLOCK), F32)],
        compiler_params=pltpu.CompilerParams(vmem_limit_bytes=24 * 1024 * 1024),
        cost_estimate=pl.CostEstimate(flops=2**21, bytes_accessed=6 * 2**20, transcendentals=0),
    )(rows, cols, scalars, tiles)


def spot(chunk):
    return 2 * (chunk % 4) + chunk // 4


OUT_PAIRS = [
    ((8 * k + a) * 8 + b, (8 * k + spot(b)) * 8 + a)
    for k in range(4)
    for a in range(8)
    for b in range(8)
]
BACK_PAIRS = [(dst, src) for src, dst in OUT_PAIRS]
CORE_PAIRS = [(s, s ^ 1) for s in range(32)]
SAME_CORE = [[2 * i + c for i in range(16)] for c in range(2)]


def swap_core(x):
    return lax.ppermute(x, "section", CORE_PAIRS)


def exchange(x, axis, groups=None):
    return lax.all_to_all(x, axis, 0, 0, tiled=False, axis_index_groups=groups)


def body(
    features, cotangent, degrees, blocks, block_rows, block_cols, block_count, w_self, w_neigh
):
    rep = lax.axis_index("rep")
    core = lax.axis_index("section") % 2
    chunk = lax.dynamic_index_in_dim(features.reshape(8, 64, 256), rep, 0, keepdims=False)
    with jax.named_scope("spread_features"):
        turned = lax.ppermute(chunk, ("section", "rep"), OUT_PAIRS)
    scalars = jnp.stack([block_count[0, 0], core.astype(jnp.int32)])
    dense, flipped = densify(blocks[0, 0], block_rows[0, 0], block_cols[0, 0], scalars)
    with jax.named_scope("gather_features"):
        own_columns = exchange(
            jnp.broadcast_to(turned[None], (16, 64, 256)), "section", SAME_CORE
        ).reshape(1024, 256)
        other_columns = swap_core(own_columns)
    partial = jnp.dot(dense[:, :1024], own_columns, preferred_element_type=F32) + jnp.dot(
        dense[:, 1024:], other_columns, preferred_element_type=F32
    )
    with jax.named_scope("sum_over_rep"):
        pieces = exchange(partial.astype(BF16).reshape(8, 64, 256), "rep")
    degree_value = degrees.astype(F32)
    degree_chunk = lax.dynamic_index_in_dim(degree_value.reshape(8, 64), rep, 0, keepdims=False)
    mean_chunk = (pieces.astype(F32).sum(axis=0) / degree_chunk[:, None]).astype(BF16)
    with jax.named_scope("gather_mean"):
        mean_input = exchange(jnp.broadcast_to(mean_chunk[None], (8, 64, 256)), "rep").reshape(
            512, 256
        )
    preact = jnp.dot(features, w_self, preferred_element_type=F32) + jnp.dot(
        mean_input, w_neigh, preferred_element_type=F32
    )
    sigmoid_value = jax.nn.sigmoid(preact)
    activated = (preact * sigmoid_value).astype(BF16)
    slope_value = sigmoid_value * (1.0 + preact * (1.0 - sigmoid_value))
    pre_grad = (cotangent.astype(F32) * slope_value).astype(BF16)
    down_grad = (
        lax.dot_general(pre_grad, w_neigh, (((1,), (1,)), ((), ())), preferred_element_type=F32)
        / degree_value[:, None]
    ).astype(BF16)
    self_part = lax.dot_general(
        pre_grad, w_self, (((1,), (1,)), ((), ())), preferred_element_type=F32
    )
    both = jnp.concatenate([features, mean_input], axis=1)
    grads = lax.dot_general(both, pre_grad, (((0,), (0,)), ((), ())), preferred_element_type=F32)
    grad_slice = lax.dynamic_slice_in_dim(grads, rep * 64, 64, 0).reshape(2, 32, 256)
    grad_own = lax.dynamic_index_in_dim(grad_slice, core, 0, keepdims=False)
    grad_other = lax.dynamic_index_in_dim(grad_slice, 1 - core, 0, keepdims=False)
    back_other = jnp.dot(flipped[1024:], down_grad, preferred_element_type=F32).astype(BF16)
    with jax.named_scope("pair_sum"):
        back_arrived = swap_core(back_other)
        grad_arrived = swap_core(grad_other)
    back_own = jnp.dot(flipped[:1024], down_grad, preferred_element_type=F32)
    back_own = (back_own + back_arrived.astype(F32)).astype(BF16).reshape(16, 64, 256)
    grad_own = (grad_own + grad_arrived).astype(BF16).reshape(16, 2, 256)
    with jax.named_scope("sum_over_section"):
        terms = exchange(jnp.concatenate([back_own, grad_own], axis=1), "section", SAME_CORE)
    term_sum = terms.astype(F32).sum(axis=0).astype(BF16)
    with jax.named_scope("return_panels"):
        returned = lax.ppermute(term_sum[:64], ("section", "rep"), BACK_PAIRS)
    with jax.named_scope("gather_grads"):
        grad_rows = exchange(jnp.broadcast_to(term_sum[None, 64:], (32, 2, 256)), "section")
    grad_rows = grad_rows.reshape(16, 2, 2, 256).transpose(1, 0, 2, 3).reshape(64, 256)
    with jax.named_scope("gather_results"):
        last = jnp.concatenate([returned, grad_rows], axis=0)
        results = exchange(jnp.broadcast_to(last[None], (8, 128, 256)), "rep").astype(F32)
    feature_grad = self_part + results[:, :64].reshape(512, 256)
    grad_self = results[:4, 64:].reshape(256, 256)
    grad_neigh = results[4:, 64:].reshape(256, 256)
    return (activated, feature_grad, grad_self, grad_neigh)


def solution(mesh):
    return jax.shard_map(
        body,
        mesh=mesh,
        in_specs=(
            P("section", None),
            P("section", None),
            P("section"),
            P("section", "rep", None, None, None),
            P("section", "rep", None),
            P("section", "rep", None),
            P("section", "rep"),
            P(),
            P(),
        ),
        out_specs=(P("section", None), P("section", None), P(), P()),
        check_vma=False,
    )
```

```python
import jax
import jax.numpy as jnp
from jax import lax
from jax.experimental import pallas as pl
from jax.experimental.pallas import tpu as pltpu
from jax.sharding import PartitionSpec as P

BLOCK = 128
F32 = jnp.float32
BF16 = jnp.bfloat16
ROWS_T = (((1,), (1,)), ((), ()))
COLS_T = (((0,), (0,)), ((), ()))
SMEM = pl.BlockSpec(memory_space=pltpu.SMEM)
VMEM = pl.BlockSpec(memory_space=pltpu.VMEM)


def section_of(z, x, core):
    return z * 8 + x * 2 + core


def device_of(z, x, core, h, y):
    return section_of(z, x, core) * 8 + h * 4 + y


def column_of(x, core):
    return x // 2, (x % 2) * 2 + core


def other_end(x_home, y_column, place):
    return (x_home + y_column + 2 - place) % 4


EVERY = [
    (z, x, core, h, y)
    for z in range(4)
    for x in range(4)
    for core in range(2)
    for h in range(2)
    for y in range(4)
]


def out_pairs(core_to):
    pairs = []
    for z, x, core, h, y in EVERY:
        h_column, y_column = column_of(x, core)
        if h == h_column:
            x_to = other_end(x, y_column, y)
            pairs.append((device_of(z, x, core, h, y), device_of(z, x_to, core_to, h, y_column)))
    return pairs


def back_pairs(flip):
    pairs = []
    for z, x, core, h, y in EVERY:
        x_home, core_home = 2 * h + y // 2, y % 2
        y_to = other_end(x_home, y, x)
        pairs.append(
            (device_of(z, x, core, h, y), device_of(z, x_home, core_home, core ^ flip, y_to))
        )
    return pairs


CORE_PAIRS = [(s, s ^ 1) for s in range(32)]
SAME_CORE = [[2 * i + core for i in range(16)] for core in range(2)]
SAME_Z = [[8 * z + i for i in range(8)] for z in range(4)]
SAME_H = [[4 * h + i for i in range(4)] for h in range(2)]
BOTH = ("section", "rep")


def swap_core(x):
    return lax.ppermute(x, "section", CORE_PAIRS)


def exchange(x, axis, groups=None):
    return lax.all_to_all(x, axis, 0, 0, tiled=False, axis_index_groups=groups)


def densify_kernel(rows_ref, cols_ref, scalars_ref, blocks_ref, dense_ref, flipped_ref, total):
    total[...] = jnp.zeros_like(total)
    live = scalars_ref[0]
    turn = scalars_ref[1]

    def add_slot(slot, carry):
        total[rows_ref[slot], cols_ref[slot]] += blocks_ref[slot].astype(F32)
        return carry

    lax.fori_loop(0, live, add_slot, 0)
    for j in range(16):
        place = (j // 4) * 4 + (turn + 4 - j % 4) % 4
        start = pl.multiple_of(place * BLOCK, BLOCK)
        for i in range(4):
            tile = total[i, j]
            dense_ref[i * BLOCK : (i + 1) * BLOCK, j * BLOCK : (j + 1) * BLOCK] = tile.astype(BF16)
            flipped_ref[pl.ds(start, BLOCK), i * BLOCK : (i + 1) * BLOCK] = tile.T.astype(BF16)


def densify(tiles, rows, cols, scalars):
    return pl.pallas_call(
        densify_kernel,
        out_shape=(
            jax.ShapeDtypeStruct((512, 2048), BF16),
            jax.ShapeDtypeStruct((2048, 512), BF16),
        ),
        in_specs=[SMEM, SMEM, SMEM, VMEM],
        out_specs=(VMEM, VMEM),
        scratch_shapes=[pltpu.VMEM((4, 16, BLOCK, BLOCK), F32)],
        compiler_params=pltpu.CompilerParams(vmem_limit_bytes=20 * 1024 * 1024),
        cost_estimate=pl.CostEstimate(flops=2**22, bytes_accessed=12 * 2**20, transcendentals=0),
    )(rows, cols, scalars, tiles)


def forward_kernel(scalars_ref, dense_ref, own_ref, other_ref, out_ref, columns):
    core = scalars_ref[2]
    own_start = pl.multiple_of(core * BLOCK, BLOCK)
    other_start = pl.multiple_of((1 - core) * BLOCK, BLOCK)
    columns[:, pl.ds(own_start, BLOCK)] = own_ref[...]
    columns[:, pl.ds(other_start, BLOCK)] = other_ref[...]
    out_ref[...] = jnp.dot(dense_ref[...], columns[...], preferred_element_type=F32).astype(BF16)


def forward_product(scalars, dense, own, other):
    return pl.pallas_call(
        forward_kernel,
        out_shape=jax.ShapeDtypeStruct((512, 256), BF16),
        in_specs=[SMEM, VMEM, VMEM, VMEM],
        out_specs=VMEM,
        scratch_shapes=[pltpu.VMEM((2048, 256), BF16)],
        compiler_params=pltpu.CompilerParams(vmem_limit_bytes=16 * 1024 * 1024),
    )(scalars, dense, own, other)


def middle_kernel(
    scalars_ref,
    pieces_ref,
    degrees_ref,
    features_ref,
    cotangent_ref,
    w_self_ref,
    w_neigh_ref,
    flipped_ref,
    activated_ref,
    pre_grad_ref,
    own_ref,
    other_ref,
    inputs,
    down,
):
    core = scalars_ref[2]
    y = scalars_ref[3]
    own_start = pl.multiple_of(core * BLOCK, BLOCK)
    other_start = pl.multiple_of((1 - core) * BLOCK, BLOCK)
    degree_value = degrees_ref[...].astype(F32)
    summed = pieces_ref[:512].astype(F32) + pieces_ref[512:].astype(F32)
    mean_input = (summed / degree_value).astype(BF16)
    features = features_ref[...]
    inputs[:, :256] = features
    inputs[:, 256:] = mean_input
    preact = jnp.dot(features, w_self_ref[...], preferred_element_type=F32) + jnp.dot(
        mean_input, w_neigh_ref[...], preferred_element_type=F32
    )
    sigmoid_value = jax.nn.sigmoid(preact)
    activated_ref[...] = (preact * sigmoid_value).astype(BF16)
    slope_value = sigmoid_value * (1.0 + preact * (1.0 - sigmoid_value))
    pre_grad = (cotangent_ref[...].astype(F32) * slope_value).astype(BF16)
    pre_grad_ref[...] = pre_grad
    down[...] = (
        lax.dot_general(pre_grad, w_neigh_ref[...], ROWS_T, preferred_element_type=F32)
        / degree_value
    ).astype(BF16)
    flipped = flipped_ref[...]
    other_ref[:2048] = jnp.dot(
        flipped, down[:, pl.ds(other_start, BLOCK)], preferred_element_type=F32
    ).astype(BF16)
    own_ref[:2048] = jnp.dot(
        flipped, down[:, pl.ds(own_start, BLOCK)], preferred_element_type=F32
    )
    mine = inputs[:, pl.ds(pl.multiple_of(y * BLOCK, BLOCK), BLOCK)]
    other_ref[2048:] = lax.dot_general(
        mine,
        pre_grad_ref[:, pl.ds(other_start, BLOCK)],
        COLS_T,
        preferred_element_type=F32,
    ).astype(BF16)
    own_ref[2048:] = lax.dot_general(
        mine,
        pre_grad_ref[:, pl.ds(own_start, BLOCK)],
        COLS_T,
        preferred_element_type=F32,
    )


def middle(scalars, pieces, degrees, features, cotangent, w_self, w_neigh, flipped):
    return pl.pallas_call(
        middle_kernel,
        out_shape=(
            jax.ShapeDtypeStruct((512, 256), BF16),
            jax.ShapeDtypeStruct((512, 256), BF16),
            jax.ShapeDtypeStruct((2176, 128), F32),
            jax.ShapeDtypeStruct((2176, 128), BF16),
        ),
        in_specs=[SMEM] + [VMEM] * 7,
        out_specs=(VMEM,) * 4,
        scratch_shapes=[pltpu.VMEM((512, 512), BF16), pltpu.VMEM((512, 256), BF16)],
        compiler_params=pltpu.CompilerParams(vmem_limit_bytes=24 * 1024 * 1024),
    )(scalars, pieces, degrees, features, cotangent, w_self, w_neigh, flipped)


def body(
    features, cotangent, degrees, blocks, block_rows, block_cols, block_count, w_self, w_neigh
):
    section = lax.axis_index("section")
    rep = lax.axis_index("rep")
    x, core = (section // 2) % 4, section % 2
    h, y = rep // 4, rep % 4
    with jax.named_scope("spread_features"):
        y_column = (x % 2) * 2 + core
        block = lax.dynamic_index_in_dim(
            features.reshape(4, BLOCK, 256), other_end(x, y_column, y), 0, keepdims=False
        )
        arrived = [
            lax.ppermute(block[:, c * BLOCK : (c + 1) * BLOCK], BOTH, out_pairs(c))
            for c in range(2)
        ]
        chunk = jnp.where(core == 0, arrived[0], arrived[1])
    scalars = jnp.stack([block_count[0, 0], (2 * h + y // 2 + y + 2) % 4, core, y])
    scalars = scalars.astype(jnp.int32)
    dense, flipped = densify(blocks[0, 0], block_rows[0, 0], block_cols[0, 0], scalars)
    chunk, dense, flipped = lax.optimization_barrier((chunk, dense, flipped))
    with jax.named_scope("gather_features"):
        own_columns = exchange(
            jnp.broadcast_to(chunk[None], (16, BLOCK, BLOCK)), "section", SAME_CORE
        ).reshape(2048, BLOCK)
        other_columns = swap_core(own_columns)
    partial = forward_product(scalars, dense, own_columns, other_columns)
    with jax.named_scope("sum_over_y"):
        terms = exchange(partial.reshape(4, BLOCK, 256), "rep", SAME_H)
        partial = terms.astype(F32).sum(axis=0).astype(BF16)
    with jax.named_scope("gather_over_rep"):
        pieces = exchange(jnp.broadcast_to(partial[None], (8, BLOCK, 256)), "rep")
    activated, pre_grad, own, other = middle(
        scalars,
        pieces.reshape(1024, 256),
        degrees[:, None],
        features,
        cotangent,
        w_self,
        w_neigh,
        flipped,
    )
    with jax.named_scope("pair_sum"):
        both = (own + swap_core(other).astype(F32)).astype(BF16)
        grad_part = jnp.broadcast_to(both[2048:].reshape(1, 4, 32, 128), (4, 4, 32, 128))
        send = jnp.concatenate(
            [both[:2048].reshape(16, BLOCK, BLOCK), grad_part.reshape(16, 32, BLOCK)], axis=1
        )
    with jax.named_scope("sum_over_section"):
        total = exchange(send, "section", SAME_CORE).astype(F32).sum(axis=0).astype(BF16)
    with jax.named_scope("return_panels"):
        halves = [lax.ppermute(total[:BLOCK], BOTH, back_pairs(flip)) for flip in range(2)]
    with jax.named_scope("gather_grads"):
        grad_rows = exchange(
            jnp.broadcast_to(total[None, BLOCK:], (8, 32, BLOCK)), "section", SAME_Z
        )
        grad_rows = grad_rows.reshape(4, 2, 32, BLOCK).transpose(0, 2, 1, 3).reshape(BLOCK, 256)
    with jax.named_scope("gather_results"):
        returned = jnp.where(
            h == 0,
            jnp.concatenate(halves, axis=1),
            jnp.concatenate(halves[::-1], axis=1),
        )
        last = jnp.concatenate([returned, grad_rows], axis=0)
        results = exchange(jnp.broadcast_to(last[None], (4, 256, 256)), "rep", SAME_H).astype(F32)
    self_part = lax.dot_general(pre_grad, w_self, ROWS_T, preferred_element_type=F32)
    feature_grad = self_part + results[:, :BLOCK].reshape(512, 256)
    grad_self = results[:2, BLOCK:].reshape(256, 256)
    grad_neigh = results[2:, BLOCK:].reshape(256, 256)
    return (activated, feature_grad, grad_self, grad_neigh)


def solution(mesh):
    return jax.shard_map(
        body,
        mesh=mesh,
        in_specs=(
            P("section", None),
            P("section", None),
            P("section"),
            P("section", "rep", None, None, None),
            P("section", "rep", None),
            P("section", "rep", None),
            P("section", "rep"),
            P(),
            P(),
        ),
        out_specs=(P("section", None), P("section", None), P(), P()),
        check_vma=False,
    )
```

```python
import jax
import jax.numpy as jnp
from jax import lax
from jax.experimental import pallas as pl
from jax.experimental.pallas import tpu as pltpu
from jax.sharding import PartitionSpec as P

BLOCK = 128
SLOTS = 48
F32 = jnp.float32
BF16 = jnp.bfloat16
ROWS_T = (((1,), (1,)), ((), ()))
COLS_T = (((0,), (0,)), ((), ()))
SMEM = pl.BlockSpec(memory_space=pltpu.SMEM)
VMEM = pl.BlockSpec(memory_space=pltpu.VMEM)


def section_of(z, x, core):
    return z * 8 + x * 2 + core


def device_of(z, x, core, h, y):
    return section_of(z, x, core) * 8 + h * 4 + y


def column_of(x, core):
    return x // 2, (x % 2) * 2 + core


def other_end(x_home, y_column, place):
    return (x_home + y_column + 2 - place) % 4


EVERY = [
    (z, x, core, h, y)
    for z in range(4)
    for x in range(4)
    for core in range(2)
    for h in range(2)
    for y in range(4)
]


def out_pairs():
    pairs = []
    for z, x, core, h, y in EVERY:
        h_column, y_column = column_of(x, core)
        if h == h_column:
            x_to = other_end(x, y_column, y)
            pairs.append((device_of(z, x, core, h, y), device_of(z, x_to, core, h, y_column)))
    return pairs


SPLIT_PAIRS = [
    (device_of(z, x, y % 2, h, y), device_of(z, x, 1 - y % 2, h, y))
    for z, x, core, h, y in EVERY
    if core == 0
]
CORE_PAIRS = [(s, s ^ 1) for s in range(32)]
SAME_CORE = [[2 * i + core for i in range(16)] for core in range(2)]
SAME_Z = [[8 * z + i for i in range(8)] for z in range(4)]
SAME_H = [[4 * h + i for i in range(4)] for h in range(2)]
BOTH = ("section", "rep")


def swap_core(x):
    return lax.ppermute(x, "section", CORE_PAIRS)


def exchange(x, axis, groups=None):
    return lax.all_to_all(x, axis, 0, 0, tiled=False, axis_index_groups=groups)


def densify_kernel(slots_ref, blocks_hbm, dense_ref, flipped_ref, blocks, total, arrived):
    copy = pltpu.make_async_copy(blocks_hbm, blocks, arrived)
    copy.start()
    total[...] = jnp.zeros_like(total)
    copy.wait()

    def add_slot(slot, carry):
        total[slots_ref[slot], slots_ref[SLOTS + slot]] += blocks[slot].astype(F32)
        return carry

    lax.fori_loop(0, slots_ref[2 * SLOTS], add_slot, 0)
    for i in range(4):
        for j in range(16):
            tile = total[i, j]
            rows, cols = pl.ds(i * BLOCK, BLOCK), pl.ds(j * BLOCK, BLOCK)
            dense_ref[rows, cols] = tile.astype(BF16)
            flipped_ref[cols, rows] = tile.T.astype(BF16)


def densify(tiles, slots):
    return pl.pallas_call(
        densify_kernel,
        out_shape=(
            jax.ShapeDtypeStruct((512, 2048), BF16),
            jax.ShapeDtypeStruct((2048, 512), BF16),
        ),
        in_specs=[SMEM, pl.BlockSpec(memory_space=pltpu.HBM)],
        out_specs=(VMEM, VMEM),
        scratch_shapes=[
            pltpu.VMEM((SLOTS, BLOCK, BLOCK), BF16),
            pltpu.VMEM((4, 16, BLOCK, BLOCK), F32),
            pltpu.SemaphoreType.DMA,
        ],
        compiler_params=pltpu.CompilerParams(vmem_limit_bytes=56 * 1024 * 1024),
        cost_estimate=pl.CostEstimate(flops=2**22, bytes_accessed=12 * 2**20, transcendentals=0),
    )(slots, tiles)


def forward_kernel(scalars_ref, dense_ref, own_ref, other_ref, out_ref, columns):
    core = scalars_ref[0]
    own_start = pl.multiple_of(core * BLOCK, BLOCK)
    other_start = pl.multiple_of((1 - core) * BLOCK, BLOCK)
    columns[:, pl.ds(own_start, BLOCK)] = own_ref[...]
    columns[:, pl.ds(other_start, BLOCK)] = other_ref[...]
    out_ref[...] = jnp.dot(dense_ref[...], columns[...], preferred_element_type=F32).astype(BF16)


def forward_product(scalars, dense, own, other):
    return pl.pallas_call(
        forward_kernel,
        out_shape=jax.ShapeDtypeStruct((512, 256), BF16),
        in_specs=[SMEM, VMEM, VMEM, VMEM],
        out_specs=VMEM,
        scratch_shapes=[pltpu.VMEM((2048, 256), BF16)],
        compiler_params=pltpu.CompilerParams(vmem_limit_bytes=16 * 1024 * 1024),
    )(scalars, dense, own, other)


def middle_kernel(
    scalars_ref,
    pieces_ref,
    degrees_ref,
    features_ref,
    cotangent_ref,
    w_self_ref,
    w_neigh_ref,
    flipped_ref,
    activated_ref,
    pre_grad_ref,
    own_ref,
    other_ref,
    inputs,
    down,
    slices,
):
    core = scalars_ref[0]
    rep = scalars_ref[1]
    degree_value = degrees_ref[...]
    summed = pieces_ref[:512].astype(F32) + pieces_ref[512:].astype(F32)
    mean_input = (summed / degree_value).astype(BF16)
    features = features_ref[...]
    inputs[:, :256] = features
    inputs[:, 256:] = mean_input
    preact = jnp.dot(features, w_self_ref[...], preferred_element_type=F32) + jnp.dot(
        mean_input, w_neigh_ref[...], preferred_element_type=F32
    )
    sigmoid_value = jax.nn.sigmoid(preact)
    activated_ref[...] = (preact * sigmoid_value).astype(BF16)
    slope_value = sigmoid_value * (1.0 + preact * (1.0 - sigmoid_value))
    pre_grad = (cotangent_ref[...].astype(F32) * slope_value).astype(BF16)
    pre_grad_ref[...] = pre_grad
    down[...] = (
        lax.dot_general(pre_grad, w_neigh_ref[...], ROWS_T, preferred_element_type=F32)
        / degree_value
    ).astype(BF16)
    first = core == 0
    for i in range(8):
        rows = pl.ds(i * 256, 256)
        term = jnp.dot(flipped_ref[rows, :], down[...], preferred_element_type=F32)
        left, right = term[:, :BLOCK], term[:, BLOCK:]
        own_ref[rows, :] = jnp.where(first, left, right)
        other_ref[rows, :] = jnp.where(first, right, left).astype(BF16)
    pair_start = pl.multiple_of(rep // 2 * BLOCK, BLOCK)
    slices[...] = lax.dot_general(
        inputs[:, pl.ds(pair_start, BLOCK)], pre_grad, COLS_T, preferred_element_type=F32
    )
    mine = slices[pl.ds(pl.multiple_of(rep % 2 * 64, 64), 64), :]
    left, right = mine[:, :BLOCK], mine[:, BLOCK:]
    own_ref[2048:] = jnp.where(first, left, right)
    other_ref[2048:] = jnp.where(first, right, left).astype(BF16)


def middle(scalars, pieces, degrees, features, cotangent, w_self, w_neigh, flipped):
    return pl.pallas_call(
        middle_kernel,
        out_shape=(
            jax.ShapeDtypeStruct((512, 256), BF16),
            jax.ShapeDtypeStruct((512, 256), BF16),
            jax.ShapeDtypeStruct((2112, 128), F32),
            jax.ShapeDtypeStruct((2112, 128), BF16),
        ),
        in_specs=[SMEM] + [VMEM] * 7,
        out_specs=(VMEM,) * 4,
        scratch_shapes=[
            pltpu.VMEM((512, 512), BF16),
            pltpu.VMEM((512, 256), BF16),
            pltpu.VMEM((BLOCK, 256), F32),
        ],
        compiler_params=pltpu.CompilerParams(vmem_limit_bytes=24 * 1024 * 1024),
    )(scalars, pieces, degrees, features, cotangent, w_self, w_neigh, flipped)


def finish_kernel(results_ref, pre_grad_ref, w_self_ref, feature_ref, self_ref, neigh_ref):
    self_part = lax.dot_general(
        pre_grad_ref[...], w_self_ref[...], ROWS_T, preferred_element_type=F32
    )
    for x in range(4):
        rows = pl.ds(x * BLOCK, BLOCK)
        for core in range(2):
            cols = pl.ds(core * BLOCK, BLOCK)
            place = 2 * x + core
            feature_ref[rows, cols] = self_part[
                x * BLOCK : (x + 1) * BLOCK, core * BLOCK : (core + 1) * BLOCK
            ] + results_ref[place, :BLOCK].astype(F32)
            for part in range(8):
                target = self_ref if part < 4 else neigh_ref
                piece = results_ref[place, BLOCK + part * 16 : BLOCK + part * 16 + 16]
                target[pl.ds(part % 4 * 64 + x * 16, 16), cols] = piece.astype(F32)


def finish(results, pre_grad, w_self):
    return pl.pallas_call(
        finish_kernel,
        out_shape=(
            jax.ShapeDtypeStruct((512, 256), F32),
            jax.ShapeDtypeStruct((256, 256), F32),
            jax.ShapeDtypeStruct((256, 256), F32),
        ),
        in_specs=[VMEM] * 3,
        out_specs=(VMEM,) * 3,
        compiler_params=pltpu.CompilerParams(vmem_limit_bytes=16 * 1024 * 1024),
    )(results, pre_grad, w_self)


def body(
    features, cotangent, degrees, blocks, block_rows, block_cols, block_count, w_self, w_neigh
):
    section = lax.axis_index("section")
    rep = lax.axis_index("rep")
    x, core = (section // 2) % 4, section % 2
    y = rep % 4
    first = core == 0
    with jax.named_scope("spread_features"):
        y_column = (x % 2) * 2 + core
        block = lax.dynamic_index_in_dim(
            features.reshape(4, BLOCK, 256), other_end(x, y_column, y), 0, keepdims=False
        )
        block = lax.ppermute(block, BOTH, out_pairs())
    slots = jnp.concatenate([block_rows[0, 0], block_cols[0, 0], block_count[0]])
    dense, flipped = densify(blocks[0, 0], slots)
    degree_column = degrees.astype(F32)[:, None]
    block, dense, flipped, degree_column = lax.optimization_barrier(
        (block, dense, flipped, degree_column)
    )
    with jax.named_scope("split_features"):
        left, right = block[:, :BLOCK], block[:, BLOCK:]
        handed = lax.ppermute(jnp.where(first, right, left), BOTH, SPLIT_PAIRS)
        chunk = jnp.where(core == y % 2, jnp.where(first, left, right), handed)
    with jax.named_scope("gather_features"):
        own_columns = exchange(
            jnp.broadcast_to(chunk[None], (16, BLOCK, BLOCK)), "section", SAME_CORE
        ).reshape(2048, BLOCK)
        other_columns = swap_core(own_columns)
    scalars = jnp.stack([core, rep]).astype(jnp.int32)
    partial = forward_product(scalars, dense, own_columns, other_columns)
    with jax.named_scope("sum_over_y"):
        terms = exchange(partial.reshape(4, BLOCK, 256), "rep", SAME_H)
        partial = terms.astype(F32).sum(axis=0).astype(BF16)
    with jax.named_scope("gather_over_rep"):
        pieces = exchange(jnp.broadcast_to(partial[None], (8, BLOCK, 256)), "rep")
    activated, pre_grad, own, other = middle(
        scalars,
        pieces.reshape(1024, 256),
        degree_column,
        features,
        cotangent,
        w_self,
        w_neigh,
        flipped,
    )
    with jax.named_scope("pair_sum"):
        both = (own + swap_core(other).astype(F32)).astype(BF16)
        grad_part = jnp.broadcast_to(both[2048:].reshape(1, 4, 16, BLOCK), (4, 4, 16, BLOCK))
        send = jnp.concatenate(
            [both[:2048].reshape(16, BLOCK, BLOCK), grad_part.reshape(16, 16, BLOCK)], axis=1
        )
    with jax.named_scope("sum_over_section"):
        total = exchange(send, "section", SAME_CORE).astype(F32).sum(axis=0).astype(BF16)
    with jax.named_scope("gather_sums"):
        sums = exchange(jnp.broadcast_to(total[None], (8, BLOCK + 16, BLOCK)), "rep")
    with jax.named_scope("return_panels"):
        grad_rows = jnp.broadcast_to(
            sums[:, BLOCK:].reshape(1, BLOCK, BLOCK), (8, BLOCK, BLOCK)
        )
        results = exchange(
            jnp.concatenate([sums[:, :BLOCK], grad_rows], axis=1), "section", SAME_Z
        )
    feature_grad, grad_self, grad_neigh = finish(results, pre_grad, w_self)
    return (activated, feature_grad, grad_self, grad_neigh)


def solution(mesh):
    return jax.shard_map(
        body,
        mesh=mesh,
        in_specs=(
            P("section", None),
            P("section", None),
            P("section"),
            P("section", "rep", None, None, None),
            P("section", "rep", None),
            P("section", "rep", None),
            P("section", "rep"),
            P(),
            P(),
        ),
        out_specs=(P("section", None), P("section", None), P(), P()),
        check_vma=False,
    )
```

```python
import jax
import jax.numpy as jnp
from jax import lax
from jax.experimental import pallas as pl
from jax.experimental.pallas import tpu as pltpu
from jax.sharding import PartitionSpec as P

BLOCK = 128
HALF = 64
F32 = jnp.float32
BF16 = jnp.bfloat16
ROWS_T = (((1,), (1,)), ((), ()))
COLS_T = (((0,), (0,)), ((), ()))
SMEM = pl.BlockSpec(memory_space=pltpu.SMEM)
VMEM = pl.BlockSpec(memory_space=pltpu.VMEM)

CORE_PAIRS = [(s, s ^ 1) for s in range(32)]
HALF_PAIRS = [(r, r ^ 4) for r in range(8)]
Z_PAIRS = [(s, s ^ 16) for s in range(32)]
SAME_CORE = [[2 * i + core for i in range(16)] for core in range(2)]
SAME_XC = [[8 * z + i for z in range(4)] for i in range(8)]
SAME_ZC = [[8 * z + 2 * x + core for x in range(4)] for z in range(4) for core in range(2)]
SAME_Z = [[8 * z + i for i in range(8)] for z in range(4)]
SAME_H = [[4 * h + i for i in range(4)] for h in range(2)]


def other_end(x_home, y_column, place):
    return (x_home + y_column + 2 - place) % 4


def out_pairs(core_to):
    pairs = []
    for z in range(4):
        for x in range(4):
            for core in range(2):
                h, y_column = x // 2, (x % 2) * 2 + core
                for y in range(4):
                    source = (8 * z + 2 * x + core) * 8 + 4 * h + y
                    x_to = other_end(x, y_column, y)
                    target = (8 * (z ^ core_to) + 2 * x_to + core_to) * 8 + 4 * h + y_column
                    pairs.append((source, target))
    return pairs


def swap_core(x):
    return lax.ppermute(x, "section", CORE_PAIRS)


def exchange(x, axis, groups=None):
    return lax.all_to_all(x, axis, 0, 0, tiled=False, axis_index_groups=groups)


def spread(x, count):
    return jnp.broadcast_to(x[None], (count, *x.shape))


def add_up(terms):
    parts = [terms[i].astype(F32) for i in range(terms.shape[0])]
    while len(parts) > 1:
        parts = [parts[i] + parts[i + 1] for i in range(0, len(parts), 2)]
    return parts[0].astype(BF16)


def densify_kernel(rows_ref, cols_ref, count_ref, blocks_ref, dense_ref, flipped_ref, total):
    total[...] = jnp.zeros_like(total)

    def add_slot(slot, carry):
        total[rows_ref[slot], cols_ref[slot]] += blocks_ref[slot].astype(F32)
        return carry

    lax.fori_loop(0, count_ref[0, 0], add_slot, 0)
    for i in range(4):
        for j in range(16):
            tile = total[i, j]
            rows, cols = pl.ds(i * BLOCK, BLOCK), pl.ds(j * BLOCK, BLOCK)
            dense_ref[rows, cols] = tile.astype(BF16)
            flipped_ref[cols, rows] = tile.T.astype(BF16)


def densify(tiles, rows, cols, count):
    return pl.pallas_call(
        densify_kernel,
        out_shape=(
            jax.ShapeDtypeStruct((512, 2048), BF16),
            jax.ShapeDtypeStruct((2048, 512), BF16),
        ),
        in_specs=[SMEM, SMEM, SMEM, VMEM],
        out_specs=(VMEM, VMEM),
        scratch_shapes=[pltpu.VMEM((4, 16, BLOCK, BLOCK), F32)],
        compiler_params=pltpu.CompilerParams(vmem_limit_bytes=20 * 1024 * 1024),
        cost_estimate=pl.CostEstimate(flops=2**22, bytes_accessed=12 * 2**20, transcendentals=0),
    )(rows, cols, count, tiles)


def forward_kernel(scalars_ref, dense_ref, own_ref, other_ref, out_ref, columns):
    panel = scalars_ref[2]
    for x in range(4):
        for pair in range(2):
            place = (2 * x + pair) * BLOCK
            own_start = (panel ^ (2 * pair)) * 512 + x * BLOCK
            other_start = (panel ^ (2 * pair) ^ 1) * 512 + x * BLOCK
            columns[pl.ds(pl.multiple_of(own_start, BLOCK), BLOCK), :] = own_ref[
                place : place + BLOCK, :
            ]
            columns[pl.ds(pl.multiple_of(other_start, BLOCK), BLOCK), :] = other_ref[
                place : place + BLOCK, :
            ]
    out_ref[...] = jnp.dot(dense_ref[...], columns[...], preferred_element_type=F32).astype(BF16)


def forward_product(scalars, dense, own, other):
    return pl.pallas_call(
        forward_kernel,
        out_shape=jax.ShapeDtypeStruct((512, 256), BF16),
        in_specs=[SMEM, VMEM, VMEM, VMEM],
        out_specs=VMEM,
        scratch_shapes=[pltpu.VMEM((2048, 256), BF16)],
        compiler_params=pltpu.CompilerParams(vmem_limit_bytes=16 * 1024 * 1024),
    )(scalars, dense, own, other)


def middle_kernel(
    scalars_ref,
    pieces_ref,
    degrees_ref,
    features_ref,
    cotangent_ref,
    w_self_ref,
    w_neigh_ref,
    flipped_ref,
    activated_ref,
    pre_grad_ref,
    own_ref,
    other_ref,
    inputs,
    divisor,
    down,
    slices,
):
    first = scalars_ref[0] == 0
    rep = scalars_ref[1]
    degree_rows = degrees_ref[...].astype(F32)
    for i in range(4):
        turned = jnp.broadcast_to(degree_rows[i : i + 1, :], (BLOCK, BLOCK)).T
        divisor[i * BLOCK : (i + 1) * BLOCK, :BLOCK] = turned
        divisor[i * BLOCK : (i + 1) * BLOCK, BLOCK:] = turned
    mean_input = (pieces_ref[...].astype(F32) / divisor[...]).astype(BF16)
    features = features_ref[...]
    inputs[:, :256] = features
    inputs[:, 256:] = mean_input
    preact = jnp.dot(features, w_self_ref[...], preferred_element_type=F32) + jnp.dot(
        mean_input, w_neigh_ref[...], preferred_element_type=F32
    )
    sigmoid_value = jax.nn.sigmoid(preact)
    activated_ref[...] = (preact * sigmoid_value).astype(BF16)
    slope_value = sigmoid_value * (1.0 + preact * (1.0 - sigmoid_value))
    pre_grad = (cotangent_ref[...].astype(F32) * slope_value).astype(BF16)
    pre_grad_ref[...] = pre_grad
    down[...] = (
        lax.dot_general(pre_grad, w_neigh_ref[...], ROWS_T, preferred_element_type=F32)
        / divisor[...]
    ).astype(BF16)
    for i in range(8):
        term = jnp.dot(
            flipped_ref[i * 256 : (i + 1) * 256, :], down[...], preferred_element_type=F32
        )
        for part in range(2):
            rows = pl.ds((2 * i + part) * HALF, HALF)
            top = term[part * BLOCK : part * BLOCK + HALF]
            bottom = term[part * BLOCK + HALF : (part + 1) * BLOCK]
            own_ref[rows, :] = jnp.where(first, top, bottom)
            other_ref[rows, :] = jnp.where(first, bottom, top).astype(BF16)
    pair_start = pl.multiple_of(rep // 2 * BLOCK, BLOCK)
    slices[...] = lax.dot_general(
        inputs[:, pl.ds(pair_start, BLOCK)], pre_grad, COLS_T, preferred_element_type=F32
    )
    mine = slices[pl.ds(pl.multiple_of(rep % 2 * HALF, HALF), HALF), :].reshape(4, 2, 8, 256)
    top, bottom = mine[:, 0].reshape(32, 256), mine[:, 1].reshape(32, 256)
    own_ref[1024:, :] = jnp.where(first, top, bottom)
    other_ref[1024:, :] = jnp.where(first, bottom, top).astype(BF16)


def middle(scalars, pieces, degrees, features, cotangent, w_self, w_neigh, flipped):
    return pl.pallas_call(
        middle_kernel,
        out_shape=(
            jax.ShapeDtypeStruct((512, 256), BF16),
            jax.ShapeDtypeStruct((512, 256), BF16),
            jax.ShapeDtypeStruct((1056, 256), F32),
            jax.ShapeDtypeStruct((1056, 256), BF16),
        ),
        in_specs=[SMEM] + [VMEM] * 7,
        out_specs=(VMEM,) * 4,
        scratch_shapes=[
            pltpu.VMEM((512, 512), BF16),
            pltpu.VMEM((512, 256), F32),
            pltpu.VMEM((512, 256), BF16),
            pltpu.VMEM((BLOCK, 256), F32),
        ],
        compiler_params=pltpu.CompilerParams(vmem_limit_bytes=24 * 1024 * 1024),
    )(scalars, pieces, degrees, features, cotangent, w_self, w_neigh, flipped)


def finish_kernel(results_ref, pre_grad_ref, w_self_ref, feature_ref, self_ref, neigh_ref):
    self_part = lax.dot_general(
        pre_grad_ref[...], w_self_ref[...], ROWS_T, preferred_element_type=F32
    )
    for place in range(8):
        rows = pl.ds(place * HALF, HALF)
        arrived = results_ref[place].astype(F32)
        feature_ref[rows, :] = self_part[place * HALF : (place + 1) * HALF] + arrived[:HALF]
        for part in range(8):
            target = self_ref if part < 4 else neigh_ref
            start = HALF + part * 8
            target[pl.ds(part % 4 * HALF + place * 8, 8), :] = arrived[start : start + 8]


def finish(results, pre_grad, w_self):
    return pl.pallas_call(
        finish_kernel,
        out_shape=(
            jax.ShapeDtypeStruct((512, 256), F32),
            jax.ShapeDtypeStruct((256, 256), F32),
            jax.ShapeDtypeStruct((256, 256), F32),
        ),
        in_specs=[VMEM] * 3,
        out_specs=(VMEM,) * 3,
        compiler_params=pltpu.CompilerParams(vmem_limit_bytes=16 * 1024 * 1024),
    )(results, pre_grad, w_self)


def body(
    features, cotangent, degrees, blocks, block_rows, block_cols, block_count, w_self, w_neigh
):
    section = lax.axis_index("section")
    rep = lax.axis_index("rep")
    z, x, core = section // 8, (section // 2) % 4, section % 2
    scalars = jnp.stack([core, rep, z ^ core]).astype(jnp.int32)
    with jax.named_scope("spread_features"):
        place = other_end(x, (x % 2) * 2 + core, rep % 4)
        block = lax.dynamic_index_in_dim(
            features.reshape(4, BLOCK, 256), place, 0, keepdims=False
        )
        arrived = [lax.ppermute(block, ("section", "rep"), out_pairs(c)) for c in range(2)]
        block = jnp.where(core == 0, arrived[0], arrived[1])
    with jax.named_scope("gather_features"):
        pair = jnp.stack([block, lax.ppermute(block, "section", Z_PAIRS)])
        own_columns = exchange(spread(pair, 4), "section", SAME_ZC).reshape(1024, 256)
        own_columns, count = lax.optimization_barrier((own_columns, block_count))
        other_columns = swap_core(own_columns)
    dense, flipped = densify(blocks[0, 0], block_rows[0, 0], block_cols[0, 0], count)
    partial = forward_product(scalars, dense, own_columns, other_columns)
    with jax.named_scope("sum_over_y"):
        partial = add_up(exchange(partial.reshape(4, BLOCK, 256), "rep", SAME_H))
    with jax.named_scope("sum_over_h"):
        partial = add_up(jnp.stack([partial, lax.ppermute(partial, "rep", HALF_PAIRS)]))
    with jax.named_scope("gather_over_y"):
        pieces = exchange(spread(partial, 4), "rep", SAME_H)
    activated, pre_grad, own, other = middle(
        scalars,
        pieces.reshape(512, 256),
        degrees.reshape(4, BLOCK),
        features,
        cotangent,
        w_self,
        w_neigh,
        flipped,
    )
    with jax.named_scope("pair_sum"):
        both = (own + swap_core(other).astype(F32)).astype(BF16)
        main = both[:1024].reshape(4, 4, HALF, 256).transpose(1, 0, 2, 3).reshape(4, 256, 256)
        send = jnp.concatenate([main, both[1024:].reshape(4, 8, 256)], axis=1)
    with jax.named_scope("sum_over_section"):
        send = add_up(exchange(send, "section", SAME_ZC))
        send = jnp.concatenate([send[:256].reshape(4, HALF, 256), spread(send[256:], 4)], axis=1)
        total = add_up(exchange(send, "section", SAME_XC))
        arrived = lax.ppermute(total, "rep", HALF_PAIRS)
        first = rep < 4
        total = jnp.stack([jnp.where(first, total, arrived), jnp.where(first, arrived, total)])
    with jax.named_scope("gather_sums"):
        sums = exchange(spread(total, 4), "rep", SAME_H)
        sums = sums.transpose(1, 0, 2, 3).reshape(8, 72, 256)
    with jax.named_scope("return_panels"):
        grad_rows = spread(sums[:, HALF:].reshape(HALF, 256), 8)
        results = exchange(
            jnp.concatenate([sums[:, :HALF], grad_rows], axis=1), "section", SAME_Z
        )
    feature_grad, grad_self, grad_neigh = finish(results, pre_grad, w_self)
    return (activated, feature_grad, grad_self, grad_neigh)


def solution(mesh):
    return jax.shard_map(
        body,
        mesh=mesh,
        in_specs=(
            P("section", None),
            P("section", None),
            P("section"),
            P("section", "rep", None, None, None),
            P("section", "rep", None),
            P("section", "rep", None),
            P("section", "rep"),
            P(),
            P(),
        ),
        out_specs=(P("section", None), P("section", None), P(), P()),
        check_vma=False,
    )
```

```python
import jax
import jax.numpy as jnp
from jax import lax
from jax.experimental import pallas as pl
from jax.experimental.pallas import tpu as pltpu
from jax.sharding import PartitionSpec as P

BLOCK = 128
HALF = 64
F32 = jnp.float32
BF16 = jnp.bfloat16
ROWS_T = (((1,), (1,)), ((), ()))
COLS_T = (((0,), (0,)), ((), ()))
SMEM = pl.BlockSpec(memory_space=pltpu.SMEM)
VMEM = pl.BlockSpec(memory_space=pltpu.VMEM)

CORE_PAIRS = [(s, s ^ 1) for s in range(32)]
HALF_PAIRS = [(r, r ^ 4) for r in range(8)]
NEXT_Z = [(s, s ^ 8) for s in range(32)]
Z_PAIRS = [(s, s ^ 16) for s in range(32)]
SAME_ZC = [[8 * z + 2 * x + core for x in range(4)] for z in range(4) for core in range(2)]
SAME_H = [[4 * h + i for i in range(4)] for h in range(2)]


def other_end(x_home, y_column, place):
    return (x_home + y_column + 2 - place) % 4


def out_pairs(core_to):
    pairs = []
    for z in range(4):
        for x in range(4):
            for core in range(2):
                h, y_column = x // 2, (x % 2) * 2 + core
                for y in range(4):
                    source = (8 * z + 2 * x + core) * 8 + 4 * h + y
                    x_to = other_end(x, y_column, y)
                    target = (8 * (z ^ core_to) + 2 * x_to + core_to) * 8 + 4 * h + y_column
                    pairs.append((source, target))
    return pairs


def back_pairs():
    pairs = []
    for z in range(4):
        for x in range(4):
            for core in range(2):
                for h in range(2):
                    for y in range(4):
                        source = (8 * z + 2 * x + core) * 8 + 4 * h + y
                        x_home, core_home = 2 * h + y // 2, y % 2
                        y_to = other_end(x_home, y, x)
                        target = (8 * z + 2 * x_home + core_home) * 8 + 4 * (core ^ h) + y_to
                        pairs.append((source, target))
    return pairs


def swap_core(x):
    return lax.ppermute(x, "section", CORE_PAIRS)


def exchange(x, axis, groups=None):
    return lax.all_to_all(x, axis, 0, 0, tiled=False, axis_index_groups=groups)


def spread(x, count):
    return jnp.broadcast_to(x[None], (count, *x.shape))


def add_up(terms):
    parts = [terms[i].astype(F32) for i in range(terms.shape[0])]
    while len(parts) > 1:
        parts = [parts[i] + parts[i + 1] for i in range(0, len(parts), 2)]
    return parts[0].astype(BF16)


def densify_kernel(scalars_ref, rows_ref, cols_ref, blocks_ref, dense_ref, flipped_ref, total):
    total[...] = jnp.zeros_like(total)

    def add_slot(slot, carry):
        total[rows_ref[slot], cols_ref[slot]] += blocks_ref[slot].astype(F32)
        return carry

    lax.fori_loop(0, scalars_ref[3], add_slot, 0)
    for i in range(4):
        for j in range(16):
            tile = total[i, j]
            rows, cols = pl.ds(i * BLOCK, BLOCK), pl.ds(j * BLOCK, BLOCK)
            dense_ref[rows, cols] = tile.astype(BF16)
            flipped_ref[cols, rows] = tile.T.astype(BF16)


def densify(scalars, tiles, rows, cols):
    return pl.pallas_call(
        densify_kernel,
        out_shape=(
            jax.ShapeDtypeStruct((512, 2048), BF16),
            jax.ShapeDtypeStruct((2048, 512), BF16),
        ),
        in_specs=[SMEM, SMEM, SMEM, VMEM],
        out_specs=(VMEM, VMEM),
        scratch_shapes=[pltpu.VMEM((4, 16, BLOCK, BLOCK), F32)],
        compiler_params=pltpu.CompilerParams(vmem_limit_bytes=20 * 1024 * 1024),
        cost_estimate=pl.CostEstimate(flops=2**22, bytes_accessed=12 * 2**20, transcendentals=0),
    )(scalars, rows, cols, tiles)


def forward_kernel(scalars_ref, dense_ref, own_ref, other_ref, out_ref, columns):
    panel = scalars_ref[2]
    for x in range(4):
        for pair in range(2):
            place = (2 * x + pair) * BLOCK
            own_start = (panel ^ (2 * pair)) * 512 + x * BLOCK
            other_start = (panel ^ (2 * pair) ^ 1) * 512 + x * BLOCK
            columns[pl.ds(pl.multiple_of(own_start, BLOCK), BLOCK), :] = own_ref[
                place : place + BLOCK, :
            ]
            columns[pl.ds(pl.multiple_of(other_start, BLOCK), BLOCK), :] = other_ref[
                place : place + BLOCK, :
            ]
    out_ref[...] = jnp.dot(dense_ref[...], columns[...], preferred_element_type=F32).astype(BF16)


def forward_product(scalars, dense, own, other):
    return pl.pallas_call(
        forward_kernel,
        out_shape=jax.ShapeDtypeStruct((512, 256), BF16),
        in_specs=[SMEM, VMEM, VMEM, VMEM],
        out_specs=VMEM,
        scratch_shapes=[pltpu.VMEM((2048, 256), BF16)],
        compiler_params=pltpu.CompilerParams(vmem_limit_bytes=16 * 1024 * 1024),
    )(scalars, dense, own, other)


def middle_kernel(
    scalars_ref,
    pieces_ref,
    degrees_ref,
    features_ref,
    cotangent_ref,
    w_self_ref,
    w_neigh_ref,
    flipped_ref,
    activated_ref,
    pre_grad_ref,
    own_ref,
    other_ref,
    inputs,
    divisor,
    down,
):
    first = scalars_ref[0] == 0
    rep = scalars_ref[1]
    degree_rows = degrees_ref[...].astype(F32)
    for i in range(4):
        turned = jnp.broadcast_to(degree_rows[i : i + 1, :], (BLOCK, BLOCK)).T
        divisor[i * BLOCK : (i + 1) * BLOCK, :BLOCK] = turned
        divisor[i * BLOCK : (i + 1) * BLOCK, BLOCK:] = turned
    mean_input = (pieces_ref[...].astype(F32) / divisor[...]).astype(BF16)
    features = features_ref[...]
    inputs[:, :256] = features
    inputs[:, 256:] = mean_input
    preact = jnp.dot(features, w_self_ref[...], preferred_element_type=F32) + jnp.dot(
        mean_input, w_neigh_ref[...], preferred_element_type=F32
    )
    sigmoid_value = jax.nn.sigmoid(preact)
    activated_ref[...] = (preact * sigmoid_value).astype(BF16)
    slope_value = sigmoid_value * (1.0 + preact * (1.0 - sigmoid_value))
    pre_grad = (cotangent_ref[...].astype(F32) * slope_value).astype(BF16)
    pre_grad_ref[...] = pre_grad
    down[...] = (
        lax.dot_general(pre_grad, w_neigh_ref[...], ROWS_T, preferred_element_type=F32)
        / divisor[...]
    ).astype(BF16)
    for i in range(8):
        start = pl.multiple_of(((i // 2) ^ scalars_ref[5]) * 512 + i % 2 * 256, 256)
        term = jnp.dot(
            flipped_ref[pl.ds(start, 256), :], down[...], preferred_element_type=F32
        )
        for part in range(2):
            rows = pl.ds((2 * i + part) * HALF, HALF)
            top = term[part * BLOCK : part * BLOCK + HALF]
            bottom = term[part * BLOCK + HALF : (part + 1) * BLOCK]
            own_ref[rows, :] = jnp.where(first, top, bottom)
            other_ref[rows, :] = jnp.where(first, bottom, top).astype(BF16)
    slice_start = pl.multiple_of(rep % 4 * BLOCK, BLOCK)
    term = lax.dot_general(
        inputs[:, pl.ds(slice_start, BLOCK)], pre_grad, COLS_T, preferred_element_type=F32
    )
    own_ref[1024:, :] = jnp.where(first, term[:HALF], term[HALF:])
    other_ref[1024:, :] = jnp.where(first, term[HALF:], term[:HALF]).astype(BF16)


def middle(scalars, pieces, degrees, features, cotangent, w_self, w_neigh, flipped):
    return pl.pallas_call(
        middle_kernel,
        out_shape=(
            jax.ShapeDtypeStruct((512, 256), BF16),
            jax.ShapeDtypeStruct((512, 256), BF16),
            jax.ShapeDtypeStruct((1088, 256), F32),
            jax.ShapeDtypeStruct((1088, 256), BF16),
        ),
        in_specs=[SMEM] + [VMEM] * 7,
        out_specs=(VMEM,) * 4,
        scratch_shapes=[
            pltpu.VMEM((512, 512), BF16),
            pltpu.VMEM((512, 256), F32),
            pltpu.VMEM((512, 256), BF16),
        ],
        compiler_params=pltpu.CompilerParams(vmem_limit_bytes=24 * 1024 * 1024),
    )(scalars, pieces, degrees, features, cotangent, w_self, w_neigh, flipped)


def finish_kernel(
    scalars_ref, results_ref, pre_grad_ref, w_self_ref, feature_ref, self_ref, neigh_ref
):
    self_part = lax.dot_general(
        pre_grad_ref[...], w_self_ref[...], ROWS_T, preferred_element_type=F32
    )
    for block in range(4):
        rows = slice(block * BLOCK, (block + 1) * BLOCK)
        y = (scalars_ref[4] + 4 - block) % 4
        feature_ref[rows, :] = self_part[rows] + results_ref[y, :BLOCK, :].astype(F32)
        target = self_ref if block < 2 else neigh_ref
        place = block % 2 * BLOCK
        target[place : place + BLOCK, :] = results_ref[block, BLOCK:].astype(F32)


def finish(scalars, results, pre_grad, w_self):
    return pl.pallas_call(
        finish_kernel,
        out_shape=(
            jax.ShapeDtypeStruct((512, 256), F32),
            jax.ShapeDtypeStruct((256, 256), F32),
            jax.ShapeDtypeStruct((256, 256), F32),
        ),
        in_specs=[SMEM] + [VMEM] * 3,
        out_specs=(VMEM,) * 3,
        compiler_params=pltpu.CompilerParams(vmem_limit_bytes=16 * 1024 * 1024),
    )(scalars, results, pre_grad, w_self)


def body(
    features, cotangent, degrees, blocks, block_rows, block_cols, block_count, w_self, w_neigh
):
    section = lax.axis_index("section")
    rep = lax.axis_index("rep")
    z, x, core = section // 8, (section // 2) % 4, section % 2
    y_column = (x % 2) * 2 + core
    scalars = jnp.stack([core, rep, z ^ core, block_count[0, 0], other_end(x, y_column, 0), z])
    scalars = scalars.astype(jnp.int32)
    with jax.named_scope("spread_features"):
        place = other_end(x, y_column, rep % 4)
        block = lax.dynamic_index_in_dim(
            features.reshape(4, BLOCK, 256), place, 0, keepdims=False
        )
        arrived = [lax.ppermute(block, ("section", "rep"), out_pairs(c)) for c in range(2)]
        block = jnp.where(core == 0, arrived[0], arrived[1])
        block, scalars = lax.optimization_barrier((block, scalars))
    with jax.named_scope("gather_features"):
        pair = jnp.stack([block, lax.ppermute(block, "section", Z_PAIRS)])
        own_columns = exchange(spread(pair, 4), "section", SAME_ZC).reshape(1024, 256)
        own_columns, row_slots = lax.optimization_barrier((own_columns, block_rows[0, 0]))
        other_columns = swap_core(own_columns)
    dense, flipped = densify(scalars, blocks[0, 0], row_slots, block_cols[0, 0])
    partial = forward_product(scalars, dense, own_columns, other_columns)
    with jax.named_scope("sum_over_y"):
        partial = add_up(exchange(partial.reshape(4, BLOCK, 256), "rep", SAME_H))
    with jax.named_scope("sum_over_h"):
        partial = add_up(jnp.stack([partial, lax.ppermute(partial, "rep", HALF_PAIRS)]))
    with jax.named_scope("gather_over_y"):
        pieces = exchange(spread(partial, 4), "rep", SAME_H)
    activated, pre_grad, own, other = middle(
        scalars,
        pieces.reshape(512, 256),
        degrees.reshape(4, BLOCK),
        features,
        cotangent,
        w_self,
        w_neigh,
        flipped,
    )
    with jax.named_scope("pair_sum"):
        both = (own + swap_core(other).astype(F32)).astype(BF16)
        main = both[:1024].reshape(4, 4, HALF, 256).transpose(1, 0, 2, 3).reshape(4, 256, 256)
        send = jnp.concatenate([main, spread(both[1024:], 4)], axis=1)
    with jax.named_scope("sum_over_section"):
        send = add_up(exchange(send, "section", SAME_ZC))
        main, grad_part = send[:256].reshape(2, 2, HALF, 256), send[256:]
        kept, sent = main[:, 0].reshape(BLOCK, 256), main[:, 1].reshape(BLOCK, 256)
        arrived = lax.ppermute(jnp.concatenate([sent, grad_part]), "section", NEXT_Z)
        pair = jnp.concatenate([kept, grad_part]).astype(F32) + arrived.astype(F32)
        pair = pair.astype(BF16)
        arrived = lax.ppermute(pair[HALF:], "section", Z_PAIRS)
        kept = jnp.concatenate([pair[:HALF], pair[BLOCK:]])
        total = kept.astype(F32) + arrived.astype(F32)
        total = total.astype(BF16)
    with jax.named_scope("return_panels"):
        swapped = swap_core(total)
        first = core == 0
        top, bottom = jnp.where(first, total, swapped), jnp.where(first, swapped, total)
        block = jnp.concatenate([top[:HALF], bottom[:HALF]], axis=0)
        block = lax.ppermute(block, ("section", "rep"), back_pairs())
    with jax.named_scope("gather_results"):
        last = jnp.concatenate([block, top[HALF:], bottom[HALF:]], axis=0)
        results = exchange(spread(last, 4), "rep", SAME_H)
    feature_grad, grad_self, grad_neigh = finish(scalars, results, pre_grad, w_self)
    return (activated, feature_grad, grad_self, grad_neigh)


def solution(mesh):
    return jax.shard_map(
        body,
        mesh=mesh,
        in_specs=(
            P("section", None),
            P("section", None),
            P("section"),
            P("section", "rep", None, None, None),
            P("section", "rep", None),
            P("section", "rep", None),
            P("section", "rep"),
            P(),
            P(),
        ),
        out_specs=(P("section", None), P("section", None), P(), P()),
        check_vma=False,
    )
```

```python
import jax
import jax.numpy as jnp
from jax import lax
from jax.experimental import pallas as pl
from jax.experimental.pallas import tpu as pltpu
from jax.sharding import PartitionSpec as P

BLOCK = 128
HALF = 64
F32 = jnp.float32
BF16 = jnp.bfloat16
ROWS_T = (((1,), (1,)), ((), ()))
COLS_T = (((0,), (0,)), ((), ()))
SMEM = pl.BlockSpec(memory_space=pltpu.SMEM)
VMEM = pl.BlockSpec(memory_space=pltpu.VMEM)

CORE_PAIRS = [(s, s ^ 1) for s in range(32)]
HALF_PAIRS = [(r, r ^ 4) for r in range(8)]
NEXT_Z = [(s, s ^ 8) for s in range(32)]
Z_PAIRS = [(s, s ^ 16) for s in range(32)]
SAME_ZC = [[8 * z + 2 * x + core for x in range(4)] for z in range(4) for core in range(2)]
SAME_H = [[4 * h + i for i in range(4)] for h in range(2)]


def other_end(x_home, y_column, place):
    return (x_home + y_column + 2 - place) % 4


def out_pairs():
    pairs = []
    for z in range(4):
        for x in range(4):
            for core in range(2):
                h, y_column = x // 2, (x % 2) * 2 + core
                for y in range(4):
                    for core_to in range(2):
                        source = (8 * z + 2 * x + core) * 8 + 4 * (h ^ core_to) + y
                        x_to = other_end(x, y_column, y)
                        section_to = 8 * (z ^ (2 * core_to)) + 2 * x_to + core_to
                        pairs.append((source, section_to * 8 + 4 * h + y_column))
    return pairs


def back_pairs():
    pairs = []
    for z in range(4):
        for x in range(4):
            for core in range(2):
                for h in range(2):
                    for y in range(4):
                        source = (8 * z + 2 * x + core) * 8 + 4 * h + y
                        x_home, core_home = 2 * h + y // 2, y % 2
                        y_to = other_end(x_home, y, x)
                        z_to = z ^ (2 * core)
                        target = (8 * z_to + 2 * x_home + core_home) * 8 + 4 * (core ^ h) + y_to
                        pairs.append((source, target))
    return pairs


def position():
    section, rep = lax.axis_index("section"), lax.axis_index("rep")
    return section // 8, section // 2 % 4, section % 2, rep // 4, rep % 4


def swap_core(x):
    return lax.ppermute(x, "section", CORE_PAIRS)


def exchange(x, axis, groups=None):
    return lax.all_to_all(x, axis, 0, 0, tiled=False, axis_index_groups=groups)


def spread(x, count):
    return jnp.broadcast_to(x[None], (count, *x.shape))


def add_up(terms):
    parts = [terms[i].astype(F32) for i in range(terms.shape[0])]
    while len(parts) > 1:
        parts = [parts[i] + parts[i + 1] for i in range(0, len(parts), 2)]
    return parts[0].astype(BF16)


def densify_kernel(scalars_ref, rows_ref, cols_ref, blocks_ref, dense_ref, flipped_ref, total):
    total[...] = jnp.zeros_like(total)

    def add_slot(slot, carry):
        total[rows_ref[slot], cols_ref[slot]] += blocks_ref[slot].astype(F32)
        return carry

    lax.fori_loop(0, scalars_ref[0], add_slot, 0)
    for i in range(4):
        for j in range(16):
            tile = total[i, j]
            rows, cols = pl.ds(i * BLOCK, BLOCK), pl.ds(j * BLOCK, BLOCK)
            dense_ref[rows, cols] = tile.astype(BF16)
            flipped_ref[cols, rows] = tile.T.astype(BF16)


def densify(scalars, tiles, rows, cols):
    return pl.pallas_call(
        densify_kernel,
        out_shape=(
            jax.ShapeDtypeStruct((512, 2048), BF16),
            jax.ShapeDtypeStruct((2048, 512), BF16),
        ),
        in_specs=[SMEM, SMEM, SMEM, VMEM],
        out_specs=(VMEM, VMEM),
        scratch_shapes=[pltpu.VMEM((4, 16, BLOCK, BLOCK), F32)],
        compiler_params=pltpu.CompilerParams(vmem_limit_bytes=20 * 1024 * 1024),
        cost_estimate=pl.CostEstimate(flops=2**22, bytes_accessed=12 * 2**20, transcendentals=0),
    )(scalars, rows, cols, tiles)


def forward_kernel(dense_ref, own_ref, other_ref, out_ref, columns):
    z, _, core, _, _ = position()
    panel = z ^ (2 * core)
    for x in range(4):
        for pair in range(2):
            place = (2 * x + pair) * BLOCK
            own_start = (panel ^ pair) * 512 + x * BLOCK
            other_start = (panel ^ 2 ^ pair) * 512 + x * BLOCK
            columns[pl.ds(pl.multiple_of(own_start, BLOCK), BLOCK), :] = own_ref[
                place : place + BLOCK, :
            ]
            columns[pl.ds(pl.multiple_of(other_start, BLOCK), BLOCK), :] = other_ref[
                place : place + BLOCK, :
            ]
    out_ref[...] = jnp.dot(dense_ref[...], columns[...], preferred_element_type=F32).astype(BF16)


def forward_product(dense, own, other):
    return pl.pallas_call(
        forward_kernel,
        out_shape=jax.ShapeDtypeStruct((512, 256), BF16),
        in_specs=[VMEM, VMEM, VMEM],
        out_specs=VMEM,
        scratch_shapes=[pltpu.VMEM((2048, 256), BF16)],
        compiler_params=pltpu.CompilerParams(vmem_limit_bytes=16 * 1024 * 1024),
    )(dense, own, other)


def middle_kernel(
    pieces_ref,
    degrees_ref,
    features_ref,
    cotangent_ref,
    w_self_ref,
    w_neigh_ref,
    flipped_ref,
    activated_ref,
    pre_grad_ref,
    own_ref,
    other_ref,
    inputs,
    divisor,
    down,
):
    z, _, core, _, y = position()
    first = core == 0
    degree_rows = degrees_ref[...].astype(F32)
    for i in range(4):
        turned = jnp.broadcast_to(degree_rows[i : i + 1, :], (BLOCK, BLOCK)).T
        divisor[i * BLOCK : (i + 1) * BLOCK, :BLOCK] = turned
        divisor[i * BLOCK : (i + 1) * BLOCK, BLOCK:] = turned
    mean_input = (pieces_ref[...].astype(F32) / divisor[...]).astype(BF16)
    features = features_ref[...]
    inputs[:, :256] = features
    inputs[:, 256:] = mean_input
    preact = jnp.dot(features, w_self_ref[...], preferred_element_type=F32) + jnp.dot(
        mean_input, w_neigh_ref[...], preferred_element_type=F32
    )
    sigmoid_value = jax.nn.sigmoid(preact)
    activated_ref[...] = (preact * sigmoid_value).astype(BF16)
    slope_value = sigmoid_value * (1.0 + preact * (1.0 - sigmoid_value))
    pre_grad = (cotangent_ref[...].astype(F32) * slope_value).astype(BF16)
    pre_grad_ref[...] = pre_grad
    down[...] = (
        lax.dot_general(pre_grad, w_neigh_ref[...], ROWS_T, preferred_element_type=F32)
        / divisor[...]
    ).astype(BF16)
    for i in range(8):
        start = pl.multiple_of(((i // 2) ^ z) * 512 + i % 2 * 256, 256)
        term = jnp.dot(
            flipped_ref[pl.ds(start, 256), :], down[...], preferred_element_type=F32
        )
        for part in range(2):
            rows = pl.ds((2 * i + part) * HALF, HALF)
            top = term[part * BLOCK : part * BLOCK + HALF]
            bottom = term[part * BLOCK + HALF : (part + 1) * BLOCK]
            own_ref[rows, :] = jnp.where(first, top, bottom)
            other_ref[rows, :] = jnp.where(first, bottom, top).astype(BF16)
    slice_start = pl.multiple_of(y * BLOCK, BLOCK)
    term = lax.dot_general(
        inputs[:, pl.ds(slice_start, BLOCK)], pre_grad, COLS_T, preferred_element_type=F32
    )
    own_ref[1024:, :] = jnp.where(first, term[:HALF], term[HALF:])
    other_ref[1024:, :] = jnp.where(first, term[HALF:], term[:HALF]).astype(BF16)


def middle(pieces, degrees, features, cotangent, w_self, w_neigh, flipped):
    return pl.pallas_call(
        middle_kernel,
        out_shape=(
            jax.ShapeDtypeStruct((512, 256), BF16),
            jax.ShapeDtypeStruct((512, 256), BF16),
            jax.ShapeDtypeStruct((1088, 256), F32),
            jax.ShapeDtypeStruct((1088, 256), BF16),
        ),
        in_specs=[VMEM] * 7,
        out_specs=(VMEM,) * 4,
        scratch_shapes=[
            pltpu.VMEM((512, 512), BF16),
            pltpu.VMEM((512, 256), F32),
            pltpu.VMEM((512, 256), BF16),
        ],
        compiler_params=pltpu.CompilerParams(vmem_limit_bytes=24 * 1024 * 1024),
    )(pieces, degrees, features, cotangent, w_self, w_neigh, flipped)


def finish_kernel(results_ref, pre_grad_ref, w_self_ref, feature_ref, self_ref, neigh_ref):
    _, x, core, _, _ = position()
    last = other_end(x, x % 2 * 2 + core, 0)
    self_part = lax.dot_general(
        pre_grad_ref[...], w_self_ref[...], ROWS_T, preferred_element_type=F32
    )
    for block in range(4):
        rows = slice(block * BLOCK, (block + 1) * BLOCK)
        y = (last + 4 - block) % 4
        feature_ref[rows, :] = self_part[rows] + results_ref[y, :BLOCK, :].astype(F32)
        target = self_ref if block < 2 else neigh_ref
        place = block % 2 * BLOCK
        target[place : place + BLOCK, :] = results_ref[block, BLOCK:].astype(F32)


def finish(results, pre_grad, w_self):
    return pl.pallas_call(
        finish_kernel,
        out_shape=(
            jax.ShapeDtypeStruct((512, 256), F32),
            jax.ShapeDtypeStruct((256, 256), F32),
            jax.ShapeDtypeStruct((256, 256), F32),
        ),
        in_specs=[VMEM] * 3,
        out_specs=(VMEM,) * 3,
        compiler_params=pltpu.CompilerParams(vmem_limit_bytes=16 * 1024 * 1024),
    )(results, pre_grad, w_self)


def body(
    features, cotangent, degrees, blocks, block_rows, block_cols, block_count, w_self, w_neigh
):
    z, x, core, h, y = position()
    y_column = x % 2 * 2 + core
    scalars = jnp.stack([block_count[0, 0], core.astype(jnp.int32)])
    with jax.named_scope("spread_features"):
        place = other_end(x, y_column, y)
        block = lax.dynamic_index_in_dim(
            features.reshape(4, BLOCK, 256), place, 0, keepdims=False
        )
        block = lax.ppermute(block, ("section", "rep"), out_pairs())
        block, scalars = lax.optimization_barrier((block, scalars))
    with jax.named_scope("gather_features"):
        pair = jnp.stack([block, lax.ppermute(block, "section", NEXT_Z)])
        own_columns = exchange(spread(pair, 4), "section", SAME_ZC).reshape(1024, 256)
        own_columns, row_slots = lax.optimization_barrier((own_columns, block_rows[0, 0]))
        other_columns = swap_core(own_columns)
    dense, flipped = densify(scalars, blocks[0, 0], row_slots, block_cols[0, 0])
    partial = forward_product(dense, own_columns, other_columns)
    with jax.named_scope("sum_over_y"):
        partial = add_up(exchange(partial.reshape(4, BLOCK, 256), "rep", SAME_H))
    with jax.named_scope("sum_over_h"):
        partial = add_up(jnp.stack([partial, lax.ppermute(partial, "rep", HALF_PAIRS)]))
    with jax.named_scope("gather_over_y"):
        pieces = exchange(spread(partial, 4), "rep", SAME_H)
    activated, pre_grad, own, other = middle(
        pieces.reshape(512, 256),
        degrees.reshape(4, BLOCK),
        features,
        cotangent,
        w_self,
        w_neigh,
        flipped,
    )
    with jax.named_scope("pair_sum"):
        both = (own + swap_core(other).astype(F32)).astype(BF16)
        main = both[:1024].reshape(4, 4, HALF, 256).transpose(1, 0, 2, 3).reshape(4, 256, 256)
        send = jnp.concatenate([main, spread(both[1024:], 4)], axis=1)
    with jax.named_scope("sum_over_section"):
        send = add_up(exchange(send, "section", SAME_ZC))
        main, grad_part = send[:256].reshape(2, 2, HALF, 256), send[256:]
        kept, sent = main[:, 0].reshape(BLOCK, 256), main[:, 1].reshape(BLOCK, 256)
        arrived = lax.ppermute(jnp.concatenate([sent, grad_part]), "section", NEXT_Z)
        pair = jnp.concatenate([kept, grad_part]).astype(F32) + arrived.astype(F32)
        pair = pair.astype(BF16)
        turned = jnp.concatenate([pair[HALF:BLOCK], pair[:HALF], pair[BLOCK:]])
        arrived = lax.ppermute(turned, "section", Z_PAIRS)
        total = (pair.astype(F32) + arrived.astype(F32)).astype(BF16)
    with jax.named_scope("return_panels"):
        first = core == 0
        kept = jnp.where(first, total[:HALF], total[HALF:BLOCK])
        given = jnp.where(first, total[HALF:BLOCK], total[:HALF])
        swapped = swap_core(jnp.concatenate([given, total[BLOCK:]]))
        kept = jnp.concatenate([kept, total[BLOCK:]])
        top, bottom = jnp.where(first, kept, swapped), jnp.where(first, swapped, kept)
        block = jnp.concatenate([top[:HALF], bottom[:HALF]], axis=0)
        block = lax.ppermute(block, ("section", "rep"), back_pairs())
    with jax.named_scope("gather_results"):
        last = jnp.concatenate([block, top[HALF:], bottom[HALF:]], axis=0)
        results = exchange(spread(last, 4), "rep", SAME_H)
    feature_grad, grad_self, grad_neigh = finish(results, pre_grad, w_self)
    return (activated, feature_grad, grad_self, grad_neigh)


def solution(mesh):
    return jax.shard_map(
        body,
        mesh=mesh,
        in_specs=(
            P("section", None),
            P("section", None),
            P("section"),
            P("section", "rep", None, None, None),
            P("section", "rep", None),
            P("section", "rep", None),
            P("section", "rep"),
            P(),
            P(),
        ),
        out_specs=(P("section", None), P("section", None), P(), P()),
        check_vma=False,
    )
```

```python
import jax
import jax.numpy as jnp
from jax import lax
from jax.experimental import pallas as pl
from jax.experimental.pallas import tpu as pltpu
from jax.sharding import PartitionSpec as P

BLOCK = 128
HALF = 64
F32 = jnp.float32
BF16 = jnp.bfloat16
ROWS_T = (((1,), (1,)), ((), ()))
COLS_T = (((0,), (0,)), ((), ()))
SMEM = pl.BlockSpec(memory_space=pltpu.SMEM)
VMEM = pl.BlockSpec(memory_space=pltpu.VMEM)

CORE_PAIRS = [(s, s ^ 1) for s in range(32)]
HALF_PAIRS = [(r, r ^ 4) for r in range(8)]
NEXT_Z = [(s, s ^ 8) for s in range(32)]
ACROSS = [(s, s ^ 17) for s in range(32)]
SAME_ZC = [[8 * z + 2 * x + core for x in range(4)] for z in range(4) for core in range(2)]
SAME_H = [[4 * h + i for i in range(4)] for h in range(2)]


def other_end(x_home, y_column, place):
    return (x_home + y_column + 2 - place) % 4


def out_pairs():
    pairs = []
    for z in range(4):
        for x in range(4):
            for core in range(2):
                h, y_column = x // 2, (x % 2) * 2 + core
                for y in range(4):
                    for core_to in range(2):
                        source = (8 * z + 2 * x + core) * 8 + 4 * (h ^ core_to) + y
                        x_to = other_end(x, y_column, y)
                        section_to = 8 * (z ^ (2 * core_to)) + 2 * x_to + core_to
                        pairs.append((source, section_to * 8 + 4 * h + y_column))
    return pairs


def back_pairs():
    pairs = []
    for z in range(4):
        for x in range(4):
            for core in range(2):
                for h in range(2):
                    for y in range(4):
                        source = (8 * z + 2 * x + core) * 8 + 4 * h + y
                        x_home, core_home = 2 * h + y // 2, y % 2
                        y_to = other_end(x_home, y, x)
                        z_to = z ^ (2 * core)
                        target = (8 * z_to + 2 * x_home + core_home) * 8 + 4 * (core ^ h) + y_to
                        pairs.append((source, target))
    return pairs


def position():
    section, rep = lax.axis_index("section"), lax.axis_index("rep")
    return section // 8, section // 2 % 4, section % 2, rep // 4, rep % 4


def swap_core(x):
    return lax.ppermute(x, "section", CORE_PAIRS)


def exchange(x, axis, groups=None):
    return lax.all_to_all(x, axis, 0, 0, tiled=False, axis_index_groups=groups)


def spread(x, count):
    return jnp.broadcast_to(x[None], (count, *x.shape))


def add_up(terms):
    parts = [terms[i].astype(F32) for i in range(terms.shape[0])]
    while len(parts) > 1:
        parts = [parts[i] + parts[i + 1] for i in range(0, len(parts), 2)]
    return parts[0].astype(BF16)


def densify_kernel(scalars_ref, rows_ref, cols_ref, blocks_ref, dense_ref, flipped_ref, total):
    total[...] = jnp.zeros_like(total)

    def add_slot(slot, carry):
        total[rows_ref[slot], cols_ref[slot]] += blocks_ref[slot].astype(F32)
        return carry

    lax.fori_loop(0, scalars_ref[0], add_slot, 0)
    for i in range(4):
        for j in range(16):
            tile = total[i, j]
            rows, cols = pl.ds(i * BLOCK, BLOCK), pl.ds(j * BLOCK, BLOCK)
            dense_ref[rows, cols] = tile.astype(BF16)
            flipped_ref[cols, rows] = tile.T.astype(BF16)


def densify(scalars, tiles, rows, cols):
    return pl.pallas_call(
        densify_kernel,
        out_shape=(
            jax.ShapeDtypeStruct((512, 2048), BF16),
            jax.ShapeDtypeStruct((2048, 512), BF16),
        ),
        in_specs=[SMEM, SMEM, SMEM, VMEM],
        out_specs=(VMEM, VMEM),
        scratch_shapes=[pltpu.VMEM((4, 16, BLOCK, BLOCK), F32)],
        compiler_params=pltpu.CompilerParams(vmem_limit_bytes=20 * 1024 * 1024),
        cost_estimate=pl.CostEstimate(flops=2**22, bytes_accessed=12 * 2**20, transcendentals=0),
    )(scalars, rows, cols, tiles)


def forward_kernel(dense_ref, own_ref, other_ref, out_ref, columns):
    z, _, core, _, _ = position()
    panel = z ^ (2 * core)
    for x in range(4):
        for pair in range(2):
            place = (2 * x + pair) * BLOCK
            own_start = (panel ^ pair) * 512 + x * BLOCK
            other_start = (panel ^ 2 ^ pair) * 512 + x * BLOCK
            columns[pl.ds(pl.multiple_of(own_start, BLOCK), BLOCK), :] = own_ref[
                place : place + BLOCK, :
            ]
            columns[pl.ds(pl.multiple_of(other_start, BLOCK), BLOCK), :] = other_ref[
                place : place + BLOCK, :
            ]
    out_ref[...] = jnp.dot(dense_ref[...], columns[...], preferred_element_type=F32).astype(BF16)


def forward_product(dense, own, other):
    return pl.pallas_call(
        forward_kernel,
        out_shape=jax.ShapeDtypeStruct((512, 256), BF16),
        in_specs=[VMEM, VMEM, VMEM],
        out_specs=VMEM,
        scratch_shapes=[pltpu.VMEM((2048, 256), BF16)],
        compiler_params=pltpu.CompilerParams(vmem_limit_bytes=16 * 1024 * 1024),
    )(dense, own, other)


def middle_kernel(
    pieces_ref,
    degrees_ref,
    features_ref,
    cotangent_ref,
    w_self_ref,
    w_neigh_ref,
    flipped_ref,
    activated_ref,
    pre_grad_ref,
    own_ref,
    other_ref,
    inputs,
    divisor,
    down,
):
    z, _, core, _, y = position()
    first = core == z // 2
    degree_rows = degrees_ref[...].astype(F32)
    for i in range(4):
        turned = jnp.broadcast_to(degree_rows[i : i + 1, :], (BLOCK, BLOCK)).T
        divisor[i * BLOCK : (i + 1) * BLOCK, :BLOCK] = turned
        divisor[i * BLOCK : (i + 1) * BLOCK, BLOCK:] = turned
    mean_input = (pieces_ref[...].astype(F32) / divisor[...]).astype(BF16)
    features = features_ref[...]
    inputs[:, :256] = features
    inputs[:, 256:] = mean_input
    preact = jnp.dot(features, w_self_ref[...], preferred_element_type=F32) + jnp.dot(
        mean_input, w_neigh_ref[...], preferred_element_type=F32
    )
    sigmoid_value = jax.nn.sigmoid(preact)
    activated_ref[...] = (preact * sigmoid_value).astype(BF16)
    slope_value = sigmoid_value * (1.0 + preact * (1.0 - sigmoid_value))
    pre_grad = (cotangent_ref[...].astype(F32) * slope_value).astype(BF16)
    pre_grad_ref[...] = pre_grad
    down[...] = (
        lax.dot_general(pre_grad, w_neigh_ref[...], ROWS_T, preferred_element_type=F32)
        / divisor[...]
    ).astype(BF16)
    panel = z ^ (2 * core)
    for pair in range(2):
        for part in range(2):
            rows = pl.ds(pair * 512 + part * 256, 256)
            own_start = pl.multiple_of((panel ^ pair) * 512 + part * 256, 256)
            other_start = pl.multiple_of((panel ^ 2 ^ pair) * 512 + part * 256, 256)
            own_ref[rows, :] = jnp.dot(
                flipped_ref[pl.ds(own_start, 256), :], down[...], preferred_element_type=F32
            )
            other_ref[rows, :] = jnp.dot(
                flipped_ref[pl.ds(other_start, 256), :], down[...], preferred_element_type=F32
            ).astype(BF16)
    slice_start = pl.multiple_of(y * BLOCK, BLOCK)
    term = lax.dot_general(
        inputs[:, pl.ds(slice_start, BLOCK)], pre_grad, COLS_T, preferred_element_type=F32
    )
    own_ref[1024:, :] = jnp.where(first, term[:HALF], term[HALF:])
    other_ref[1024:, :] = jnp.where(first, term[HALF:], term[:HALF]).astype(BF16)


def middle(pieces, degrees, features, cotangent, w_self, w_neigh, flipped):
    return pl.pallas_call(
        middle_kernel,
        out_shape=(
            jax.ShapeDtypeStruct((512, 256), BF16),
            jax.ShapeDtypeStruct((512, 256), BF16),
            jax.ShapeDtypeStruct((1088, 256), F32),
            jax.ShapeDtypeStruct((1088, 256), BF16),
        ),
        in_specs=[VMEM] * 7,
        out_specs=(VMEM,) * 4,
        scratch_shapes=[
            pltpu.VMEM((512, 512), BF16),
            pltpu.VMEM((512, 256), F32),
            pltpu.VMEM((512, 256), BF16),
        ],
        compiler_params=pltpu.CompilerParams(vmem_limit_bytes=24 * 1024 * 1024),
    )(pieces, degrees, features, cotangent, w_self, w_neigh, flipped)


def finish_kernel(results_ref, pre_grad_ref, w_self_ref, feature_ref, self_ref, neigh_ref):
    _, x, core, _, _ = position()
    last = other_end(x, x % 2 * 2 + core, 0)
    self_part = lax.dot_general(
        pre_grad_ref[...], w_self_ref[...], ROWS_T, preferred_element_type=F32
    )
    for block in range(4):
        rows = slice(block * BLOCK, (block + 1) * BLOCK)
        y = (last + 4 - block) % 4
        feature_ref[rows, :] = self_part[rows] + results_ref[y, :BLOCK, :].astype(F32)
        target = self_ref if block < 2 else neigh_ref
        place = block % 2 * BLOCK
        target[place : place + BLOCK, :] = results_ref[block, BLOCK:].astype(F32)


def finish(results, pre_grad, w_self):
    return pl.pallas_call(
        finish_kernel,
        out_shape=(
            jax.ShapeDtypeStruct((512, 256), F32),
            jax.ShapeDtypeStruct((256, 256), F32),
            jax.ShapeDtypeStruct((256, 256), F32),
        ),
        in_specs=[VMEM] * 3,
        out_specs=(VMEM,) * 3,
        compiler_params=pltpu.CompilerParams(vmem_limit_bytes=16 * 1024 * 1024),
    )(results, pre_grad, w_self)


def body(
    features, cotangent, degrees, blocks, block_rows, block_cols, block_count, w_self, w_neigh
):
    z, x, core, h, y = position()
    y_column = x % 2 * 2 + core
    scalars = jnp.stack([block_count[0, 0], core.astype(jnp.int32)])
    with jax.named_scope("spread_features"):
        place = other_end(x, y_column, y)
        block = lax.dynamic_index_in_dim(
            features.reshape(4, BLOCK, 256), place, 0, keepdims=False
        )
        block = lax.ppermute(block, ("section", "rep"), out_pairs())
        block, scalars = lax.optimization_barrier((block, scalars))
    with jax.named_scope("gather_features"):
        pair = jnp.stack([block, lax.ppermute(block, "section", NEXT_Z)])
        own_columns = exchange(spread(pair, 4), "section", SAME_ZC).reshape(1024, 256)
        own_columns, row_slots = lax.optimization_barrier((own_columns, block_rows[0, 0]))
        other_columns = swap_core(own_columns)
    dense, flipped = densify(scalars, blocks[0, 0], row_slots, block_cols[0, 0])
    partial = forward_product(dense, own_columns, other_columns)
    with jax.named_scope("sum_over_y"):
        partial = add_up(exchange(partial.reshape(4, BLOCK, 256), "rep", SAME_H))
    with jax.named_scope("sum_over_h"):
        partial = add_up(jnp.stack([partial, lax.ppermute(partial, "rep", HALF_PAIRS)]))
    with jax.named_scope("gather_over_y"):
        pieces = exchange(spread(partial, 4), "rep", SAME_H)
    activated, pre_grad, own, other = middle(
        pieces.reshape(512, 256),
        degrees.reshape(4, BLOCK),
        features,
        cotangent,
        w_self,
        w_neigh,
        flipped,
    )
    with jax.named_scope("pair_sum"):
        both = (own + swap_core(other).astype(F32)).astype(BF16)
        main = both[:1024].reshape(2, 4, BLOCK, 256).transpose(1, 0, 2, 3).reshape(4, 256, 256)
        send = jnp.concatenate([main, spread(both[1024:], 4)], axis=1)
    with jax.named_scope("sum_over_section"):
        total = add_up(exchange(send, "section", SAME_ZC))
        arrived = lax.ppermute(total[BLOCK:], "section", NEXT_Z)
        kept = jnp.concatenate([total[:BLOCK], total[256:]])
        total = (kept.astype(F32) + arrived.astype(F32)).astype(BF16)
        arrived = lax.ppermute(total, "section", ACROSS)
        total = (total.astype(F32) + arrived.astype(F32)).astype(BF16)
    with jax.named_scope("return_panels"):
        block = lax.ppermute(total[:BLOCK], ("section", "rep"), back_pairs())
        own_rows, other_rows = total[BLOCK:], swap_core(total[BLOCK:])
    with jax.named_scope("gather_results"):
        first = core == z // 2
        top, bottom = jnp.where(first, own_rows, other_rows), jnp.where(first, other_rows, own_rows)
        last = jnp.concatenate([block, top, bottom], axis=0)
        results = exchange(spread(last, 4), "rep", SAME_H)
    feature_grad, grad_self, grad_neigh = finish(results, pre_grad, w_self)
    return (activated, feature_grad, grad_self, grad_neigh)


def solution(mesh):
    return jax.shard_map(
        body,
        mesh=mesh,
        in_specs=(
            P("section", None),
            P("section", None),
            P("section"),
            P("section", "rep", None, None, None),
            P("section", "rep", None),
            P("section", "rep", None),
            P("section", "rep"),
            P(),
            P(),
        ),
        out_specs=(P("section", None), P("section", None), P(), P()),
        check_vma=False,
    )
```

```python
import jax
import jax.numpy as jnp
from jax import lax
from jax.experimental import pallas as pl
from jax.experimental.pallas import tpu as pltpu
from jax.sharding import PartitionSpec as P

BLOCK = 128
HALF = 64
F32 = jnp.float32
BF16 = jnp.bfloat16
ROWS_T = (((1,), (1,)), ((), ()))
COLS_T = (((0,), (0,)), ((), ()))
SMEM = pl.BlockSpec(memory_space=pltpu.SMEM)
VMEM = pl.BlockSpec(memory_space=pltpu.VMEM)

CORE_PAIRS = [(s, s ^ 1) for s in range(32)]
HALF_PAIRS = [(r, r ^ 4) for r in range(8)]
NEXT_Z = [(s, s ^ 8) for s in range(32)]
ACROSS = [(s, s ^ 17) for s in range(32)]
SAME_ZC = [[8 * z + 2 * x + core for x in range(4)] for z in range(4) for core in range(2)]
SAME_H = [[4 * h + i for i in range(4)] for h in range(2)]


def other_end(x_home, y_column, place):
    return (x_home + y_column + 2 - place) % 4


def out_pairs():
    pairs = []
    for z in range(4):
        for x in range(4):
            for core in range(2):
                h, y_column = x // 2, (x % 2) * 2 + core
                for y in range(4):
                    for core_to in range(2):
                        source = (8 * z + 2 * x + core) * 8 + 4 * (h ^ core_to) + y
                        x_to = other_end(x, y_column, y)
                        section_to = 8 * (z ^ (2 * core_to)) + 2 * x_to + core_to
                        pairs.append((source, section_to * 8 + 4 * h + y_column))
    return pairs


def back_pairs():
    pairs = []
    for z in range(4):
        for x in range(4):
            for core in range(2):
                for h in range(2):
                    for y in range(4):
                        source = (8 * z + 2 * x + core) * 8 + 4 * h + y
                        x_home, core_home = 2 * h + y // 2, y % 2
                        y_to = other_end(x_home, y, x)
                        z_to = z ^ (2 * core)
                        target = (8 * z_to + 2 * x_home + core_home) * 8 + 4 * (core ^ h) + y_to
                        pairs.append((source, target))
    return pairs


def position():
    section, rep = lax.axis_index("section"), lax.axis_index("rep")
    return section // 8, section // 2 % 4, section % 2, rep // 4, rep % 4


def swap_core(x):
    return lax.ppermute(x, "section", CORE_PAIRS)


def exchange(x, axis, groups=None):
    return lax.all_to_all(x, axis, 0, 0, tiled=False, axis_index_groups=groups)


def spread(x, count):
    return jnp.broadcast_to(x[None], (count, *x.shape))


def add_up(terms):
    parts = [terms[i].astype(F32) for i in range(terms.shape[0])]
    while len(parts) > 1:
        parts = [parts[i] + parts[i + 1] for i in range(0, len(parts), 2)]
    return parts[0].astype(BF16)


def densify_kernel(scalars_ref, rows_ref, cols_ref, blocks_ref, dense_ref, total):
    total[...] = jnp.zeros_like(total)

    def add_slot(slot, carry):
        total[rows_ref[slot], cols_ref[slot]] += blocks_ref[slot].astype(F32)
        return carry

    lax.fori_loop(0, scalars_ref[0], add_slot, 0)
    for i in range(4):
        for j in range(16):
            tile = total[i, j]
            rows, cols = pl.ds(i * BLOCK, BLOCK), pl.ds(j * BLOCK, BLOCK)
            dense_ref[rows, cols] = tile.astype(BF16)


def densify(scalars, tiles, rows, cols):
    return pl.pallas_call(
        densify_kernel,
        out_shape=jax.ShapeDtypeStruct((512, 2048), BF16),
        in_specs=[SMEM, SMEM, SMEM, VMEM],
        out_specs=VMEM,
        scratch_shapes=[pltpu.VMEM((4, 16, BLOCK, BLOCK), F32)],
        compiler_params=pltpu.CompilerParams(vmem_limit_bytes=20 * 1024 * 1024),
        cost_estimate=pl.CostEstimate(flops=2**22, bytes_accessed=12 * 2**20, transcendentals=0),
    )(scalars, rows, cols, tiles)


def forward_kernel(dense_ref, own_ref, other_ref, out_ref, columns):
    z, _, core, _, _ = position()
    panel = z ^ (2 * core)
    for x in range(4):
        for pair in range(2):
            place = (2 * x + pair) * BLOCK
            own_start = (panel ^ pair) * 512 + x * BLOCK
            other_start = (panel ^ 2 ^ pair) * 512 + x * BLOCK
            columns[pl.ds(pl.multiple_of(own_start, BLOCK), BLOCK), :] = own_ref[
                place : place + BLOCK, :
            ]
            columns[pl.ds(pl.multiple_of(other_start, BLOCK), BLOCK), :] = other_ref[
                place : place + BLOCK, :
            ]
    out_ref[...] = jnp.dot(dense_ref[...], columns[...], preferred_element_type=F32).astype(BF16)


def forward_product(dense, own, other):
    return pl.pallas_call(
        forward_kernel,
        out_shape=jax.ShapeDtypeStruct((512, 256), BF16),
        in_specs=[VMEM, VMEM, VMEM],
        out_specs=VMEM,
        scratch_shapes=[pltpu.VMEM((2048, 256), BF16)],
        compiler_params=pltpu.CompilerParams(vmem_limit_bytes=16 * 1024 * 1024),
    )(dense, own, other)


def prepare_kernel(
    dense_ref, degrees_ref, features_ref, w_self_ref, flipped_ref, scale_ref, base_ref
):
    for i in range(4):
        for j in range(16):
            rows, cols = pl.ds(i * BLOCK, BLOCK), pl.ds(j * BLOCK, BLOCK)
            flipped_ref[cols, rows] = dense_ref[rows, cols].astype(F32).T.astype(BF16)
    inverse = 1.0 / degrees_ref[...].astype(F32)
    for i in range(4):
        turned = jnp.broadcast_to(inverse[i : i + 1, :], (BLOCK, BLOCK)).T
        scale_ref[i * BLOCK : (i + 1) * BLOCK, :] = turned
    base_ref[...] = jnp.dot(features_ref[...], w_self_ref[...], preferred_element_type=F32)


def prepare(dense, degrees, features, w_self):
    return pl.pallas_call(
        prepare_kernel,
        out_shape=(
            jax.ShapeDtypeStruct((2048, 512), BF16),
            jax.ShapeDtypeStruct((512, BLOCK), F32),
            jax.ShapeDtypeStruct((512, 256), F32),
        ),
        in_specs=[VMEM] * 4,
        out_specs=(VMEM,) * 3,
        compiler_params=pltpu.CompilerParams(vmem_limit_bytes=16 * 1024 * 1024),
        cost_estimate=pl.CostEstimate(flops=2**27, bytes_accessed=5 * 2**20, transcendentals=0),
    )(dense, degrees, features, w_self)


def middle_kernel(
    pieces_ref,
    scale_ref,
    base_ref,
    features_ref,
    cotangent_ref,
    w_neigh_ref,
    flipped_ref,
    preact_ref,
    pre_grad_ref,
    own_ref,
    other_ref,
    inputs,
    down,
):
    z, _, core, _, y = position()
    first = core == z // 2
    scale = jnp.concatenate([scale_ref[...], scale_ref[...]], axis=1)
    mean_input = (pieces_ref[...].astype(F32) * scale).astype(BF16)
    inputs[:, :256] = features_ref[...]
    inputs[:, 256:] = mean_input
    preact = base_ref[...] + jnp.dot(mean_input, w_neigh_ref[...], preferred_element_type=F32)
    sigmoid_value = jax.nn.sigmoid(preact)
    preact_ref[...] = preact
    slope_value = sigmoid_value * (1.0 + preact * (1.0 - sigmoid_value))
    pre_grad = (cotangent_ref[...].astype(F32) * slope_value).astype(BF16)
    pre_grad_ref[...] = pre_grad
    down[...] = (
        lax.dot_general(pre_grad, w_neigh_ref[...], ROWS_T, preferred_element_type=F32)
        * scale
    ).astype(BF16)
    panel = z ^ (2 * core)
    for pair in range(2):
        for part in range(2):
            rows = pl.ds(pair * 512 + part * 256, 256)
            own_start = pl.multiple_of((panel ^ pair) * 512 + part * 256, 256)
            other_start = pl.multiple_of((panel ^ 2 ^ pair) * 512 + part * 256, 256)
            own_ref[rows, :] = jnp.dot(
                flipped_ref[pl.ds(own_start, 256), :], down[...], preferred_element_type=F32
            )
            other_ref[rows, :] = jnp.dot(
                flipped_ref[pl.ds(other_start, 256), :], down[...], preferred_element_type=F32
            ).astype(BF16)
    slice_start = pl.multiple_of(y * BLOCK, BLOCK)
    term = lax.dot_general(
        inputs[:, pl.ds(slice_start, BLOCK)], pre_grad, COLS_T, preferred_element_type=F32
    )
    own_ref[1024:, :] = jnp.where(first, term[:HALF], term[HALF:])
    other_ref[1024:, :] = jnp.where(first, term[HALF:], term[:HALF]).astype(BF16)


def middle(*operands):
    return pl.pallas_call(
        middle_kernel,
        out_shape=(
            jax.ShapeDtypeStruct((512, 256), F32),
            jax.ShapeDtypeStruct((512, 256), BF16),
            jax.ShapeDtypeStruct((1088, 256), F32),
            jax.ShapeDtypeStruct((1088, 256), BF16),
        ),
        in_specs=[VMEM] * 7,
        out_specs=(VMEM,) * 4,
        scratch_shapes=[
            pltpu.VMEM((512, 512), BF16),
            pltpu.VMEM((512, 256), BF16),
        ],
        compiler_params=pltpu.CompilerParams(vmem_limit_bytes=24 * 1024 * 1024),
    )(*operands)


def activate_kernel(preact_ref, activated_ref):
    preact = preact_ref[...]
    activated_ref[...] = (preact * jax.nn.sigmoid(preact)).astype(BF16)


def activate(preact):
    return pl.pallas_call(
        activate_kernel,
        out_shape=jax.ShapeDtypeStruct((512, 256), BF16),
        in_specs=[VMEM],
        out_specs=VMEM,
        compiler_params=pltpu.CompilerParams(vmem_limit_bytes=16 * 1024 * 1024),
        cost_estimate=pl.CostEstimate(flops=2**21, bytes_accessed=2**20, transcendentals=2**17),
    )(preact)


def feature_kernel(results_ref, pre_grad_ref, w_self_ref, feature_ref):
    _, x, core, _, _ = position()
    last = other_end(x, x % 2 * 2 + core, 0)
    self_part = lax.dot_general(
        pre_grad_ref[...], w_self_ref[...], ROWS_T, preferred_element_type=F32
    )
    for block in range(4):
        rows = slice(block * BLOCK, (block + 1) * BLOCK)
        y = (last + 4 - block) % 4
        feature_ref[rows, :] = self_part[rows] + results_ref[y, :BLOCK, :].astype(F32)


def finish_features(results, pre_grad, w_self):
    return pl.pallas_call(
        feature_kernel,
        out_shape=jax.ShapeDtypeStruct((512, 256), F32),
        in_specs=[VMEM] * 3,
        out_specs=VMEM,
        compiler_params=pltpu.CompilerParams(vmem_limit_bytes=16 * 1024 * 1024),
        cost_estimate=pl.CostEstimate(flops=2**27, bytes_accessed=2**21, transcendentals=0),
    )(results, pre_grad, w_self)


def grad_kernel(own_ref, other_ref, self_ref, neigh_ref):
    z, _, core, _, _ = position()
    first = core == z // 2
    for y in range(4):
        own, other = own_ref[y].astype(F32), other_ref[y].astype(F32)
        target = self_ref if y < 2 else neigh_ref
        start = y % 2 * BLOCK
        target[start : start + HALF, :] = jnp.where(first, own, other)
        target[start + HALF : start + BLOCK, :] = jnp.where(first, other, own)


def finish_grads(own, other):
    return pl.pallas_call(
        grad_kernel,
        out_shape=(
            jax.ShapeDtypeStruct((256, 256), F32),
            jax.ShapeDtypeStruct((256, 256), F32),
        ),
        in_specs=[VMEM] * 2,
        out_specs=(VMEM,) * 2,
        compiler_params=pltpu.CompilerParams(vmem_limit_bytes=16 * 1024 * 1024),
    )(own, other)


def body(
    features, cotangent, degrees, blocks, block_rows, block_cols, block_count, w_self, w_neigh
):
    z, x, core, h, y = position()
    y_column = x % 2 * 2 + core
    scalars = jnp.stack([block_count[0, 0], core.astype(jnp.int32)])
    with jax.named_scope("spread_features"):
        place = other_end(x, y_column, y)
        block = lax.dynamic_index_in_dim(
            features.reshape(4, BLOCK, 256), place, 0, keepdims=False
        )
        block = lax.ppermute(block, ("section", "rep"), out_pairs())
        block, scalars = lax.optimization_barrier((block, scalars))
    with jax.named_scope("gather_features"):
        pair = jnp.stack([block, lax.ppermute(block, "section", NEXT_Z)])
        own_columns = exchange(spread(pair, 4), "section", SAME_ZC).reshape(1024, 256)
        own_columns, row_slots = lax.optimization_barrier((own_columns, block_rows[0, 0]))
        other_columns = swap_core(own_columns)
    dense = densify(scalars, blocks[0, 0], row_slots, block_cols[0, 0])
    partial = forward_product(dense, own_columns, other_columns)
    with jax.named_scope("sum_over_y"):
        partial = add_up(exchange(partial.reshape(4, BLOCK, 256), "rep", SAME_H))
    with jax.named_scope("sum_over_h"):
        partial, degree_rows = lax.optimization_barrier((partial, degrees.reshape(4, BLOCK)))
        arrived = lax.ppermute(partial, "rep", HALF_PAIRS)
        flipped, scale, base = prepare(dense, degree_rows, features, w_self)
        partial = add_up(jnp.stack([partial, arrived]))
    with jax.named_scope("gather_over_y"):
        partial, flipped = lax.optimization_barrier((partial, flipped))
        pieces = exchange(spread(partial, 4), "rep", SAME_H)
    preact, pre_grad, own, other = middle(
        pieces.reshape(512, 256), scale, base, features, cotangent, w_neigh, flipped
    )
    with jax.named_scope("pair_sum"):
        both = (own + swap_core(other).astype(F32)).astype(BF16)
        main = both[:1024].reshape(2, 4, BLOCK, 256).transpose(1, 0, 2, 3).reshape(4, 256, 256)
        send = jnp.concatenate([main, spread(both[1024:], 4)], axis=1)
    with jax.named_scope("sum_over_section"):
        total = add_up(exchange(send, "section", SAME_ZC))
        arrived = lax.ppermute(total[BLOCK:], "section", NEXT_Z)
        kept = jnp.concatenate([total[:BLOCK], total[256:]])
        total = (kept.astype(F32) + arrived.astype(F32)).astype(BF16)
        arrived = lax.ppermute(total, "section", ACROSS)
        total = (total.astype(F32) + arrived.astype(F32)).astype(BF16)
    with jax.named_scope("return_panels"):
        block = lax.ppermute(total[:BLOCK], ("section", "rep"), back_pairs())
        activated = activate(preact)
        block, activated = lax.optimization_barrier((block, activated))
    with jax.named_scope("gather_results"):
        last = jnp.concatenate([block, total[BLOCK:]], axis=0)
        results = exchange(spread(last, 4), "rep", SAME_H)
        own_rows = results[:, BLOCK:]
        other_rows = swap_core(own_rows)
    feature_grad = finish_features(results, pre_grad, w_self)
    grad_self, grad_neigh = finish_grads(own_rows, other_rows)
    return (activated, feature_grad, grad_self, grad_neigh)


def solution(mesh):
    return jax.shard_map(
        body,
        mesh=mesh,
        in_specs=(
            P("section", None),
            P("section", None),
            P("section"),
            P("section", "rep", None, None, None),
            P("section", "rep", None),
            P("section", "rep", None),
            P("section", "rep"),
            P(),
            P(),
        ),
        out_specs=(P("section", None), P("section", None), P(), P()),
        check_vma=False,
    )
```

```python
import jax
import jax.numpy as jnp
from jax import lax
from jax.experimental import pallas as pl
from jax.experimental.pallas import tpu as pltpu
from jax.sharding import PartitionSpec as P

BLOCK = 128
HALF = 64
F32 = jnp.float32
BF16 = jnp.bfloat16
ROWS_T = (((1,), (1,)), ((), ()))
COLS_T = (((0,), (0,)), ((), ()))
SMEM = pl.BlockSpec(memory_space=pltpu.SMEM)
VMEM = pl.BlockSpec(memory_space=pltpu.VMEM)

CORE_PAIRS = [(s, s ^ 1) for s in range(32)]
HALF_PAIRS = [(r, r ^ 4) for r in range(8)]
NEXT_Z = [(s, s ^ 8) for s in range(32)]
ACROSS = [(s, s ^ 17) for s in range(32)]
SAME_ZC = [[8 * z + 2 * x + core for x in range(4)] for z in range(4) for core in range(2)]
SAME_H = [[4 * h + i for i in range(4)] for h in range(2)]


def other_end(x_home, y_column, place):
    return (x_home + y_column + 2 - place) % 4


def out_pairs():
    pairs = []
    for z in range(4):
        for x in range(4):
            for core in range(2):
                h, y_column = x // 2, (x % 2) * 2 + core
                for y in range(4):
                    for core_to in range(2):
                        source = (8 * z + 2 * x + core) * 8 + 4 * (h ^ core_to) + y
                        x_to = other_end(x, y_column, y)
                        section_to = 8 * (z ^ (2 * core_to)) + 2 * x_to + core_to
                        pairs.append((source, section_to * 8 + 4 * h + y_column))
    return pairs


def back_pairs():
    pairs = []
    for z in range(4):
        for x in range(4):
            for core in range(2):
                for h in range(2):
                    for y in range(4):
                        source = (8 * z + 2 * x + core) * 8 + 4 * h + y
                        x_home, core_home = 2 * h + y // 2, y % 2
                        y_to = other_end(x_home, y, x)
                        z_to = z ^ (2 * core)
                        target = (8 * z_to + 2 * x_home + core_home) * 8 + 4 * (core ^ h) + y_to
                        pairs.append((source, target))
    return pairs


def position():
    section, rep = lax.axis_index("section"), lax.axis_index("rep")
    return section // 8, section // 2 % 4, section % 2, rep // 4, rep % 4


def swap_core(x):
    return lax.ppermute(x, "section", CORE_PAIRS)


def exchange(x, axis, groups=None):
    return lax.all_to_all(x, axis, 0, 0, tiled=False, axis_index_groups=groups)


def spread(x, count):
    return jnp.broadcast_to(x[None], (count, *x.shape))


def add_up(terms):
    parts = [terms[i].astype(F32) for i in range(terms.shape[0])]
    while len(parts) > 1:
        parts = [parts[i] + parts[i + 1] for i in range(0, len(parts), 2)]
    return parts[0].astype(BF16)


def densify_kernel(scalars_ref, rows_ref, cols_ref, blocks_ref, dense_ref, total):
    total[...] = jnp.zeros_like(total)

    def add_slot(slot, carry):
        total[rows_ref[slot], cols_ref[slot]] += blocks_ref[slot].astype(F32)
        return carry

    lax.fori_loop(0, scalars_ref[0], add_slot, 0)
    for i in range(4):
        for j in range(16):
            tile = total[i, j]
            rows, cols = pl.ds(i * BLOCK, BLOCK), pl.ds(j * BLOCK, BLOCK)
            dense_ref[rows, cols] = tile.astype(BF16)


def densify(scalars, tiles, rows, cols):
    return pl.pallas_call(
        densify_kernel,
        out_shape=jax.ShapeDtypeStruct((512, 2048), BF16),
        in_specs=[SMEM, SMEM, SMEM, VMEM],
        out_specs=VMEM,
        scratch_shapes=[pltpu.VMEM((4, 16, BLOCK, BLOCK), F32)],
        compiler_params=pltpu.CompilerParams(vmem_limit_bytes=20 * 1024 * 1024),
        cost_estimate=pl.CostEstimate(flops=2**22, bytes_accessed=12 * 2**20, transcendentals=0),
    )(scalars, rows, cols, tiles)


def forward_kernel(dense_ref, own_ref, other_ref, out_ref, columns):
    z, _, core, _, _ = position()
    panel = z ^ (2 * core)
    for x in range(4):
        for pair in range(2):
            place = (2 * x + pair) * BLOCK
            own_start = (panel ^ pair) * 512 + x * BLOCK
            other_start = (panel ^ 2 ^ pair) * 512 + x * BLOCK
            columns[pl.ds(pl.multiple_of(own_start, BLOCK), BLOCK), :] = own_ref[
                place : place + BLOCK, :
            ]
            columns[pl.ds(pl.multiple_of(other_start, BLOCK), BLOCK), :] = other_ref[
                place : place + BLOCK, :
            ]
    out_ref[...] = jnp.dot(dense_ref[...], columns[...], preferred_element_type=F32).astype(BF16)


def forward_product(dense, own, other):
    return pl.pallas_call(
        forward_kernel,
        out_shape=jax.ShapeDtypeStruct((512, 256), BF16),
        in_specs=[VMEM, VMEM, VMEM],
        out_specs=VMEM,
        scratch_shapes=[pltpu.VMEM((2048, 256), BF16)],
        compiler_params=pltpu.CompilerParams(vmem_limit_bytes=16 * 1024 * 1024),
    )(dense, own, other)


def prepare_kernel(
    dense_ref,
    degrees_ref,
    features_ref,
    w_self_ref,
    flipped_ref,
    scale_ref,
    chunk_scale_ref,
    base_ref,
):
    for i in range(4):
        for j in range(16):
            rows, cols = pl.ds(i * BLOCK, BLOCK), pl.ds(j * BLOCK, BLOCK)
            flipped_ref[cols, rows] = dense_ref[rows, cols].astype(F32).T.astype(BF16)
    inverse = 1.0 / degrees_ref[...].astype(F32)
    for i in range(4):
        turned = jnp.broadcast_to(inverse[i : i + 1, :], (BLOCK, BLOCK)).T
        scale_ref[i * BLOCK : (i + 1) * BLOCK, :] = turned
    _, _, _, _, y = position()
    chunk_scale = scale_ref[pl.ds(pl.multiple_of(y * BLOCK, BLOCK), BLOCK), :]
    chunk_scale_ref[...] = jnp.concatenate([chunk_scale, chunk_scale], axis=1)
    base_ref[...] = jnp.dot(features_ref[...], w_self_ref[...], preferred_element_type=F32)


def prepare(dense, degrees, features, w_self):
    return pl.pallas_call(
        prepare_kernel,
        out_shape=(
            jax.ShapeDtypeStruct((2048, 512), BF16),
            jax.ShapeDtypeStruct((512, BLOCK), F32),
            jax.ShapeDtypeStruct((BLOCK, 256), F32),
            jax.ShapeDtypeStruct((512, 256), F32),
        ),
        in_specs=[VMEM] * 4,
        out_specs=(VMEM,) * 4,
        compiler_params=pltpu.CompilerParams(vmem_limit_bytes=16 * 1024 * 1024),
        cost_estimate=pl.CostEstimate(flops=2**27, bytes_accessed=5 * 2**20, transcendentals=0),
    )(dense, degrees, features, w_self)


def transposed_product(flipped_ref, panel, down_ref, out_ref):
    for pair in range(2):
        for part in range(2):
            start = pl.multiple_of((panel ^ pair) * 512 + part * 256, 256)
            term = jnp.dot(
                flipped_ref[pl.ds(start, 256), :], down_ref[...], preferred_element_type=F32
            ).astype(out_ref.dtype)
            for x in range(2):
                place = (4 * part + 2 * x + pair) * BLOCK
                out_ref[place : place + BLOCK, :] = term[x * BLOCK : (x + 1) * BLOCK]


def own_kernel(flipped_ref, down_ref, own_ref):
    z, _, core, _, _ = position()
    transposed_product(flipped_ref, z ^ (2 * core), down_ref, own_ref)


def own_product(flipped, down):
    return pl.pallas_call(
        own_kernel,
        out_shape=jax.ShapeDtypeStruct((1024, 256), F32),
        in_specs=[VMEM, VMEM],
        out_specs=VMEM,
        compiler_params=pltpu.CompilerParams(vmem_limit_bytes=16 * 1024 * 1024),
        cost_estimate=pl.CostEstimate(flops=2**28, bytes_accessed=4 * 2**20, transcendentals=0),
    )(flipped, down)


def middle_kernel(
    mean_ref,
    scale_ref,
    base_ref,
    features_ref,
    cotangent_ref,
    w_neigh_ref,
    flipped_ref,
    preact_ref,
    pre_grad_ref,
    down_ref,
    grad_ref,
    other_ref,
    inputs,
):
    z, _, core, _, y = position()
    first = core == z // 2
    scale = jnp.concatenate([scale_ref[...], scale_ref[...]], axis=1)
    mean_input = mean_ref[...]
    inputs[:, :256] = features_ref[...]
    inputs[:, 256:] = mean_input
    preact = base_ref[...] + jnp.dot(mean_input, w_neigh_ref[...], preferred_element_type=F32)
    sigmoid_value = jax.nn.sigmoid(preact)
    preact_ref[...] = preact
    slope_value = sigmoid_value * (1.0 + preact * (1.0 - sigmoid_value))
    pre_grad = (cotangent_ref[...].astype(F32) * slope_value).astype(BF16)
    pre_grad_ref[...] = pre_grad
    down_ref[...] = (
        lax.dot_general(pre_grad, w_neigh_ref[...], ROWS_T, preferred_element_type=F32)
        * scale
    ).astype(BF16)
    transposed_product(flipped_ref, z ^ (2 * core) ^ 2, down_ref, other_ref)
    slice_start = pl.multiple_of(y * BLOCK, BLOCK)
    term = lax.dot_general(
        inputs[:, pl.ds(slice_start, BLOCK)], pre_grad, COLS_T, preferred_element_type=F32
    )
    grad_ref[...] = jnp.where(first, term[:HALF], term[HALF:])
    other_ref[1024:, :] = jnp.where(first, term[HALF:], term[:HALF]).astype(BF16)


def middle(*operands):
    return pl.pallas_call(
        middle_kernel,
        out_shape=(
            jax.ShapeDtypeStruct((512, 256), F32),
            jax.ShapeDtypeStruct((512, 256), BF16),
            jax.ShapeDtypeStruct((512, 256), BF16),
            jax.ShapeDtypeStruct((HALF, 256), F32),
            jax.ShapeDtypeStruct((1088, 256), BF16),
        ),
        in_specs=[VMEM] * 7,
        out_specs=(VMEM,) * 5,
        scratch_shapes=[
            pltpu.VMEM((512, 512), BF16),
        ],
        compiler_params=pltpu.CompilerParams(vmem_limit_bytes=24 * 1024 * 1024),
    )(*operands)


def activate_kernel(preact_ref, activated_ref):
    preact = preact_ref[...]
    activated_ref[...] = (preact * jax.nn.sigmoid(preact)).astype(BF16)


def activate(preact):
    return pl.pallas_call(
        activate_kernel,
        out_shape=jax.ShapeDtypeStruct((512, 256), BF16),
        in_specs=[VMEM],
        out_specs=VMEM,
        compiler_params=pltpu.CompilerParams(vmem_limit_bytes=16 * 1024 * 1024),
        cost_estimate=pl.CostEstimate(flops=2**21, bytes_accessed=2**20, transcendentals=2**17),
    )(preact)


def feature_kernel(results_ref, pre_grad_ref, w_self_ref, feature_ref):
    _, x, core, _, _ = position()
    last = other_end(x, x % 2 * 2 + core, 0)
    self_part = lax.dot_general(
        pre_grad_ref[...], w_self_ref[...], ROWS_T, preferred_element_type=F32
    )
    for block in range(4):
        rows = slice(block * BLOCK, (block + 1) * BLOCK)
        y = (last + 4 - block) % 4
        feature_ref[rows, :] = self_part[rows] + results_ref[y, :BLOCK, :].astype(F32)


def finish_features(results, pre_grad, w_self):
    return pl.pallas_call(
        feature_kernel,
        out_shape=jax.ShapeDtypeStruct((512, 256), F32),
        in_specs=[VMEM] * 3,
        out_specs=VMEM,
        compiler_params=pltpu.CompilerParams(vmem_limit_bytes=16 * 1024 * 1024),
        cost_estimate=pl.CostEstimate(flops=2**27, bytes_accessed=2**21, transcendentals=0),
    )(results, pre_grad, w_self)


def grad_kernel(own_ref, other_ref, self_ref, neigh_ref):
    z, _, core, _, _ = position()
    first = core == z // 2
    for y in range(4):
        own, other = own_ref[y].astype(F32), other_ref[y].astype(F32)
        target = self_ref if y < 2 else neigh_ref
        start = y % 2 * BLOCK
        target[start : start + HALF, :] = jnp.where(first, own, other)
        target[start + HALF : start + BLOCK, :] = jnp.where(first, other, own)


def finish_grads(own, other):
    return pl.pallas_call(
        grad_kernel,
        out_shape=(
            jax.ShapeDtypeStruct((256, 256), F32),
            jax.ShapeDtypeStruct((256, 256), F32),
        ),
        in_specs=[VMEM] * 2,
        out_specs=(VMEM,) * 2,
        compiler_params=pltpu.CompilerParams(vmem_limit_bytes=16 * 1024 * 1024),
    )(own, other)


def body(
    features, cotangent, degrees, blocks, block_rows, block_cols, block_count, w_self, w_neigh
):
    z, x, core, h, y = position()
    y_column = x % 2 * 2 + core
    scalars = jnp.stack([block_count[0, 0], core.astype(jnp.int32)])
    with jax.named_scope("spread_features"):
        place = other_end(x, y_column, y)
        block = lax.dynamic_index_in_dim(
            features.reshape(4, BLOCK, 256), place, 0, keepdims=False
        )
        block = lax.ppermute(block, ("section", "rep"), out_pairs())
        block, scalars = lax.optimization_barrier((block, scalars))
    with jax.named_scope("gather_features"):
        pair = jnp.stack([block, lax.ppermute(block, "section", NEXT_Z)])
        own_columns = exchange(spread(pair, 4), "section", SAME_ZC).reshape(1024, 256)
        own_columns, row_slots = lax.optimization_barrier((own_columns, block_rows[0, 0]))
        other_columns = swap_core(own_columns)
    dense = densify(scalars, blocks[0, 0], row_slots, block_cols[0, 0])
    partial = forward_product(dense, own_columns, other_columns)
    with jax.named_scope("sum_over_y"):
        partial = add_up(exchange(partial.reshape(4, BLOCK, 256), "rep", SAME_H))
    with jax.named_scope("sum_over_h"):
        partial, degree_rows = lax.optimization_barrier((partial, degrees.reshape(4, BLOCK)))
        arrived = lax.ppermute(partial, "rep", HALF_PAIRS)
        flipped, scale, chunk_scale, base = prepare(dense, degree_rows, features, w_self)
        summed = partial.astype(F32) + arrived.astype(F32)
        mean_chunk = (summed * chunk_scale).astype(BF16)
    with jax.named_scope("gather_over_y"):
        mean_chunk, flipped = lax.optimization_barrier((mean_chunk, flipped))
        mean_input = exchange(spread(mean_chunk, 4), "rep", SAME_H)
    preact, pre_grad, down, own_grad, other = middle(
        mean_input.reshape(512, 256), scale, base, features, cotangent, w_neigh, flipped
    )
    with jax.named_scope("pair_sum"):
        arrived = swap_core(other)
        own = own_product(flipped, down)
        main = (own + arrived[:1024].astype(F32)).astype(BF16).reshape(4, 256, 256)
        grad_part = (own_grad + arrived[1024:].astype(F32)).astype(BF16)
        send = jnp.concatenate([main, spread(grad_part, 4)], axis=1)
    with jax.named_scope("sum_over_section"):
        total = add_up(exchange(send, "section", SAME_ZC))
        arrived = lax.ppermute(total[BLOCK:], "section", NEXT_Z)
        kept = jnp.concatenate([total[:BLOCK], total[256:]])
        total = (kept.astype(F32) + arrived.astype(F32)).astype(BF16)
        arrived = lax.ppermute(total, "section", ACROSS)
        total = (total.astype(F32) + arrived.astype(F32)).astype(BF16)
    with jax.named_scope("return_panels"):
        block = lax.ppermute(total[:BLOCK], ("section", "rep"), back_pairs())
        activated = activate(preact)
        block, activated = lax.optimization_barrier((block, activated))
    with jax.named_scope("gather_results"):
        last = jnp.concatenate([block, total[BLOCK:]], axis=0)
        results = exchange(spread(last, 4), "rep", SAME_H)
        own_rows = results[:, BLOCK:]
        other_rows = swap_core(own_rows)
    feature_grad = finish_features(results, pre_grad, w_self)
    grad_self, grad_neigh = finish_grads(own_rows, other_rows)
    return (activated, feature_grad, grad_self, grad_neigh)


def solution(mesh):
    return jax.shard_map(
        body,
        mesh=mesh,
        in_specs=(
            P("section", None),
            P("section", None),
            P("section"),
            P("section", "rep", None, None, None),
            P("section", "rep", None),
            P("section", "rep", None),
            P("section", "rep"),
            P(),
            P(),
        ),
        out_specs=(P("section", None), P("section", None), P(), P()),
        check_vma=False,
    )
```

```python
import jax
import jax.numpy as jnp
from jax import lax
from jax.experimental import pallas as pl
from jax.experimental.pallas import tpu as pltpu
from jax.sharding import PartitionSpec as P

BLOCK = 128
HALF = 64
F32 = jnp.float32
BF16 = jnp.bfloat16
ROWS_T = (((1,), (1,)), ((), ()))
COLS_T = (((0,), (0,)), ((), ()))
SMEM = pl.BlockSpec(memory_space=pltpu.SMEM)
VMEM = pl.BlockSpec(memory_space=pltpu.VMEM)

CORE_PAIRS = [(s, s ^ 1) for s in range(32)]
HALF_PAIRS = [(r, r ^ 4) for r in range(8)]
NEXT_Z = [(s, s ^ 8) for s in range(32)]
Z_PAIRS = [(s, s ^ 16) for s in range(32)]
SAME_ZC = [[8 * z + 2 * x + core for x in range(4)] for z in range(4) for core in range(2)]
SAME_H = [[4 * h + i for i in range(4)] for h in range(2)]


def other_end(x_home, y_column, place):
    return (x_home + y_column + 2 - place) % 4


def out_pairs():
    pairs = []
    for z in range(4):
        for x in range(4):
            for core in range(2):
                h, y_column = x // 2, (x % 2) * 2 + core
                for y in range(4):
                    for core_to in range(2):
                        source = (8 * z + 2 * x + core) * 8 + 4 * (h ^ core_to) + y
                        x_to = other_end(x, y_column, y)
                        section_to = 8 * (z ^ (2 * core_to)) + 2 * x_to + core_to
                        pairs.append((source, section_to * 8 + 4 * h + y_column))
    return pairs


def back_pairs():
    pairs = []
    for z in range(4):
        for x in range(4):
            for core in range(2):
                for h in range(2):
                    for y in range(4):
                        source = (8 * z + 2 * x + core) * 8 + 4 * h + y
                        x_home, core_home = 2 * h + y // 2, y % 2
                        y_to = other_end(x_home, y, x)
                        away = core ^ (z // 2)
                        section_to = 8 * (z ^ (2 * away)) + 2 * x_home + core_home
                        pairs.append((source, section_to * 8 + 4 * (h ^ away) + y_to))
    return pairs


def position():
    section, rep = lax.axis_index("section"), lax.axis_index("rep")
    return section // 8, section // 2 % 4, section % 2, rep // 4, rep % 4


def swap_core(x):
    return lax.ppermute(x, "section", CORE_PAIRS)


def exchange(x, axis, groups=None):
    return lax.all_to_all(x, axis, 0, 0, tiled=False, axis_index_groups=groups)


def spread(x, count):
    return jnp.broadcast_to(x[None], (count, *x.shape))


def add_up(terms):
    parts = [terms[i].astype(F32) for i in range(terms.shape[0])]
    while len(parts) > 1:
        parts = [parts[i] + parts[i + 1] for i in range(0, len(parts), 2)]
    return parts[0].astype(BF16)


def densify_kernel(scalars_ref, rows_ref, cols_ref, blocks_ref, dense_ref, total):
    total[...] = jnp.zeros_like(total)

    def add_slot(slot, carry):
        total[rows_ref[slot], cols_ref[slot]] += blocks_ref[slot].astype(F32)
        return carry

    lax.fori_loop(0, scalars_ref[0], add_slot, 0)
    for i in range(4):
        for j in range(16):
            tile = total[i, j]
            rows, cols = pl.ds(i * BLOCK, BLOCK), pl.ds(j * BLOCK, BLOCK)
            dense_ref[rows, cols] = tile.astype(BF16)


def densify(scalars, tiles, rows, cols):
    return pl.pallas_call(
        densify_kernel,
        out_shape=jax.ShapeDtypeStruct((512, 2048), BF16),
        in_specs=[SMEM, SMEM, SMEM, VMEM],
        out_specs=VMEM,
        scratch_shapes=[pltpu.VMEM((4, 16, BLOCK, BLOCK), F32)],
        compiler_params=pltpu.CompilerParams(vmem_limit_bytes=20 * 1024 * 1024),
        cost_estimate=pl.CostEstimate(flops=2**22, bytes_accessed=12 * 2**20, transcendentals=0),
    )(scalars, rows, cols, tiles)


def forward_kernel(dense_ref, own_ref, other_ref, out_ref, columns):
    z, _, core, _, _ = position()
    panel = z ^ (2 * core)
    for x in range(4):
        for pair in range(2):
            place = (2 * x + pair) * BLOCK
            own_start = (panel ^ pair) * 512 + x * BLOCK
            other_start = (panel ^ 2 ^ pair) * 512 + x * BLOCK
            columns[pl.ds(pl.multiple_of(own_start, BLOCK), BLOCK), :] = own_ref[
                place : place + BLOCK, :
            ]
            columns[pl.ds(pl.multiple_of(other_start, BLOCK), BLOCK), :] = other_ref[
                place : place + BLOCK, :
            ]
    out_ref[...] = jnp.dot(dense_ref[...], columns[...], preferred_element_type=F32).astype(BF16)


def forward_product(dense, own, other):
    return pl.pallas_call(
        forward_kernel,
        out_shape=jax.ShapeDtypeStruct((512, 256), BF16),
        in_specs=[VMEM, VMEM, VMEM],
        out_specs=VMEM,
        scratch_shapes=[pltpu.VMEM((2048, 256), BF16)],
        compiler_params=pltpu.CompilerParams(vmem_limit_bytes=16 * 1024 * 1024),
    )(dense, own, other)


def prepare_kernel(
    dense_ref,
    degrees_ref,
    features_ref,
    w_self_ref,
    flipped_ref,
    scale_ref,
    chunk_scale_ref,
    base_ref,
):
    for i in range(4):
        for j in range(16):
            rows, cols = pl.ds(i * BLOCK, BLOCK), pl.ds(j * BLOCK, BLOCK)
            flipped_ref[cols, rows] = dense_ref[rows, cols].astype(F32).T.astype(BF16)
    inverse = 1.0 / degrees_ref[...].astype(F32)
    for i in range(4):
        turned = jnp.broadcast_to(inverse[i : i + 1, :], (BLOCK, BLOCK)).T
        scale_ref[i * BLOCK : (i + 1) * BLOCK, :] = turned
    _, _, _, _, y = position()
    chunk_scale = scale_ref[pl.ds(pl.multiple_of(y * BLOCK, BLOCK), BLOCK), :]
    chunk_scale_ref[...] = jnp.concatenate([chunk_scale, chunk_scale], axis=1)
    base_ref[...] = jnp.dot(features_ref[...], w_self_ref[...], preferred_element_type=F32)


def prepare(dense, degrees, features, w_self):
    return pl.pallas_call(
        prepare_kernel,
        out_shape=(
            jax.ShapeDtypeStruct((2048, 512), BF16),
            jax.ShapeDtypeStruct((512, BLOCK), F32),
            jax.ShapeDtypeStruct((BLOCK, 256), F32),
            jax.ShapeDtypeStruct((512, 256), F32),
        ),
        in_specs=[VMEM] * 4,
        out_specs=(VMEM,) * 4,
        compiler_params=pltpu.CompilerParams(vmem_limit_bytes=16 * 1024 * 1024),
        cost_estimate=pl.CostEstimate(flops=2**27, bytes_accessed=5 * 2**20, transcendentals=0),
    )(dense, degrees, features, w_self)


def transposed_product(flipped_ref, panel, down_ref, out_ref):
    for pair in range(2):
        for part in range(2):
            start = pl.multiple_of((panel ^ pair) * 512 + part * 256, 256)
            term = jnp.dot(
                flipped_ref[pl.ds(start, 256), :], down_ref[...], preferred_element_type=F32
            ).astype(out_ref.dtype)
            for x in range(2):
                place = (4 * part + 2 * x + pair) * BLOCK
                out_ref[place : place + BLOCK, :] = term[x * BLOCK : (x + 1) * BLOCK]


def own_kernel(flipped_ref, down_ref, own_ref):
    z, _, core, _, _ = position()
    transposed_product(flipped_ref, 2 * core + z % 2, down_ref, own_ref)


def own_product(flipped, down):
    return pl.pallas_call(
        own_kernel,
        out_shape=jax.ShapeDtypeStruct((1024, 256), F32),
        in_specs=[VMEM, VMEM],
        out_specs=VMEM,
        compiler_params=pltpu.CompilerParams(vmem_limit_bytes=16 * 1024 * 1024),
        cost_estimate=pl.CostEstimate(flops=2**28, bytes_accessed=4 * 2**20, transcendentals=0),
    )(flipped, down)


def middle_kernel(
    mean_ref,
    scale_ref,
    base_ref,
    features_ref,
    cotangent_ref,
    w_neigh_ref,
    flipped_ref,
    preact_ref,
    pre_grad_ref,
    down_ref,
    grad_ref,
    other_ref,
    inputs,
):
    z, _, core, _, y = position()
    first = core == 0
    scale = jnp.concatenate([scale_ref[...], scale_ref[...]], axis=1)
    mean_input = mean_ref[...]
    inputs[:, :256] = features_ref[...]
    inputs[:, 256:] = mean_input
    preact = base_ref[...] + jnp.dot(mean_input, w_neigh_ref[...], preferred_element_type=F32)
    sigmoid_value = jax.nn.sigmoid(preact)
    preact_ref[...] = preact
    slope_value = sigmoid_value * (1.0 + preact * (1.0 - sigmoid_value))
    pre_grad = (cotangent_ref[...].astype(F32) * slope_value).astype(BF16)
    pre_grad_ref[...] = pre_grad
    down_ref[...] = (
        lax.dot_general(pre_grad, w_neigh_ref[...], ROWS_T, preferred_element_type=F32)
        * scale
    ).astype(BF16)
    transposed_product(flipped_ref, (2 * core + z % 2) ^ 2, down_ref, other_ref)
    slice_start = pl.multiple_of(y * BLOCK, BLOCK)
    term = lax.dot_general(
        inputs[:, pl.ds(slice_start, BLOCK)], pre_grad, COLS_T, preferred_element_type=F32
    )
    grad_ref[...] = jnp.where(first, term[:HALF], term[HALF:])
    other_ref[1024:, :] = jnp.where(first, term[HALF:], term[:HALF]).astype(BF16)


def middle(*operands):
    return pl.pallas_call(
        middle_kernel,
        out_shape=(
            jax.ShapeDtypeStruct((512, 256), F32),
            jax.ShapeDtypeStruct((512, 256), BF16),
            jax.ShapeDtypeStruct((512, 256), BF16),
            jax.ShapeDtypeStruct((HALF, 256), F32),
            jax.ShapeDtypeStruct((1088, 256), BF16),
        ),
        in_specs=[VMEM] * 7,
        out_specs=(VMEM,) * 5,
        scratch_shapes=[
            pltpu.VMEM((512, 512), BF16),
        ],
        compiler_params=pltpu.CompilerParams(vmem_limit_bytes=24 * 1024 * 1024),
    )(*operands)


def activate_kernel(preact_ref, activated_ref):
    preact = preact_ref[...]
    activated_ref[...] = (preact * jax.nn.sigmoid(preact)).astype(BF16)


def activate(preact):
    return pl.pallas_call(
        activate_kernel,
        out_shape=jax.ShapeDtypeStruct((512, 256), BF16),
        in_specs=[VMEM],
        out_specs=VMEM,
        compiler_params=pltpu.CompilerParams(vmem_limit_bytes=16 * 1024 * 1024),
        cost_estimate=pl.CostEstimate(flops=2**21, bytes_accessed=2**20, transcendentals=2**17),
    )(preact)


def feature_kernel(results_ref, pre_grad_ref, w_self_ref, feature_ref):
    _, x, core, _, _ = position()
    last = other_end(x, x % 2 * 2 + core, 0)
    self_part = lax.dot_general(
        pre_grad_ref[...], w_self_ref[...], ROWS_T, preferred_element_type=F32
    )
    for block in range(4):
        rows = slice(block * BLOCK, (block + 1) * BLOCK)
        y = (last + 4 - block) % 4
        feature_ref[rows, :] = self_part[rows] + results_ref[y, :BLOCK, :].astype(F32)


def finish_features(results, pre_grad, w_self):
    return pl.pallas_call(
        feature_kernel,
        out_shape=jax.ShapeDtypeStruct((512, 256), F32),
        in_specs=[VMEM] * 3,
        out_specs=VMEM,
        compiler_params=pltpu.CompilerParams(vmem_limit_bytes=16 * 1024 * 1024),
        cost_estimate=pl.CostEstimate(flops=2**27, bytes_accessed=2**21, transcendentals=0),
    )(results, pre_grad, w_self)


def grad_kernel(own_ref, other_ref, self_ref, neigh_ref):
    first = position()[2] == 0
    for y in range(4):
        own, other = own_ref[y].astype(F32), other_ref[y].astype(F32)
        target = self_ref if y < 2 else neigh_ref
        start = y % 2 * BLOCK
        target[start : start + HALF, :] = jnp.where(first, own, other)
        target[start + HALF : start + BLOCK, :] = jnp.where(first, other, own)


def finish_grads(own, other):
    return pl.pallas_call(
        grad_kernel,
        out_shape=(
            jax.ShapeDtypeStruct((256, 256), F32),
            jax.ShapeDtypeStruct((256, 256), F32),
        ),
        in_specs=[VMEM] * 2,
        out_specs=(VMEM,) * 2,
        compiler_params=pltpu.CompilerParams(vmem_limit_bytes=16 * 1024 * 1024),
    )(own, other)


def body(
    features, cotangent, degrees, blocks, block_rows, block_cols, block_count, w_self, w_neigh
):
    z, x, core, h, y = position()
    y_column = x % 2 * 2 + core
    scalars = jnp.stack([block_count[0, 0], core.astype(jnp.int32)])
    with jax.named_scope("spread_features"):
        place = other_end(x, y_column, y)
        block = lax.dynamic_index_in_dim(
            features.reshape(4, BLOCK, 256), place, 0, keepdims=False
        )
        block = lax.ppermute(block, ("section", "rep"), out_pairs())
        block, scalars = lax.optimization_barrier((block, scalars))
    with jax.named_scope("gather_features"):
        pair = jnp.stack([block, lax.ppermute(block, "section", NEXT_Z)])
        own_columns = exchange(spread(pair, 4), "section", SAME_ZC).reshape(1024, 256)
        own_columns, row_slots = lax.optimization_barrier((own_columns, block_rows[0, 0]))
        other_columns = swap_core(own_columns)
    dense = densify(scalars, blocks[0, 0], row_slots, block_cols[0, 0])
    partial = forward_product(dense, own_columns, other_columns)
    with jax.named_scope("sum_over_y"):
        partial = add_up(exchange(partial.reshape(4, BLOCK, 256), "rep", SAME_H))
    with jax.named_scope("sum_over_h"):
        partial, degree_rows = lax.optimization_barrier((partial, degrees.reshape(4, BLOCK)))
        arrived = lax.ppermute(partial, "rep", HALF_PAIRS)
        flipped, scale, chunk_scale, base = prepare(dense, degree_rows, features, w_self)
        summed = partial.astype(F32) + arrived.astype(F32)
        mean_chunk = (summed * chunk_scale).astype(BF16)
    with jax.named_scope("gather_over_y"):
        mean_chunk, flipped = lax.optimization_barrier((mean_chunk, flipped))
        mean_input = exchange(spread(mean_chunk, 4), "rep", SAME_H)
    preact, pre_grad, down, own_grad, other = middle(
        mean_input.reshape(512, 256), scale, base, features, cotangent, w_neigh, flipped
    )
    with jax.named_scope("pair_sum"):
        arrived = swap_core(other)
        own = own_product(flipped, down)
        main = (own + arrived[:1024].astype(F32)).astype(BF16).reshape(4, 256, 256)
        grad_part = (own_grad + arrived[1024:].astype(F32)).astype(BF16)
        send = jnp.concatenate([main, spread(grad_part, 4)], axis=1)
    with jax.named_scope("sum_over_section"):
        total = add_up(exchange(send, "section", SAME_ZC))
        arrived = lax.ppermute(total[BLOCK:], "section", NEXT_Z)
        kept = jnp.concatenate([total[:BLOCK], total[256:]])
        total = (kept.astype(F32) + arrived.astype(F32)).astype(BF16)
        arrived = lax.ppermute(total, "section", Z_PAIRS)
        total = (total.astype(F32) + arrived.astype(F32)).astype(BF16)
    with jax.named_scope("return_panels"):
        block = lax.ppermute(total[:BLOCK], ("section", "rep"), back_pairs())
        activated = activate(preact)
        block, activated = lax.optimization_barrier((block, activated))
    with jax.named_scope("gather_results"):
        last = jnp.concatenate([block, total[BLOCK:]], axis=0)
        results = exchange(spread(last, 4), "rep", SAME_H)
        own_rows = results[:, BLOCK:]
        other_rows = swap_core(own_rows)
    feature_grad = finish_features(results, pre_grad, w_self)
    grad_self, grad_neigh = finish_grads(own_rows, other_rows)
    return (activated, feature_grad, grad_self, grad_neigh)


def solution(mesh):
    return jax.shard_map(
        body,
        mesh=mesh,
        in_specs=(
            P("section", None),
            P("section", None),
            P("section"),
            P("section", "rep", None, None, None),
            P("section", "rep", None),
            P("section", "rep", None),
            P("section", "rep"),
            P(),
            P(),
        ),
        out_specs=(P("section", None), P("section", None), P(), P()),
        check_vma=False,
    )
```

```python
import jax
import jax.numpy as jnp
from jax import lax
from jax.experimental import pallas as pl
from jax.experimental.pallas import tpu as pltpu
from jax.sharding import PartitionSpec as P

BLOCK = 128
HALF = 64
F32 = jnp.float32
BF16 = jnp.bfloat16
ROWS_T = (((1,), (1,)), ((), ()))
COLS_T = (((0,), (0,)), ((), ()))
SMEM = pl.BlockSpec(memory_space=pltpu.SMEM)
VMEM = pl.BlockSpec(memory_space=pltpu.VMEM)

CORE_PAIRS = [(s, s ^ 1) for s in range(32)]
HALF_PAIRS = [(r, r ^ 4) for r in range(8)]
NEXT_Z = [(s, s ^ 8) for s in range(32)]
Z_PAIRS = [(s, s ^ 16) for s in range(32)]
SAME_ZC = [[8 * z + 2 * x + core for x in range(4)] for z in range(4) for core in range(2)]
SAME_H = [[4 * h + i for i in range(4)] for h in range(2)]


def other_end(x_home, y_column, place):
    return (x_home + y_column + 2 - place) % 4


def out_pairs():
    pairs = []
    for z in range(4):
        for x in range(4):
            for core in range(2):
                h, y_column = x // 2, (x % 2) * 2 + core
                for y in range(4):
                    for core_to in range(2):
                        source = (8 * z + 2 * x + core) * 8 + 4 * (h ^ core_to) + y
                        x_to = other_end(x, y_column, y)
                        section_to = 8 * (z ^ (2 * core_to)) + 2 * x_to + core_to
                        pairs.append((source, section_to * 8 + 4 * h + y_column))
    return pairs


def back_pairs():
    pairs = []
    for z in range(4):
        for x in range(4):
            for core in range(2):
                for h in range(2):
                    for y in range(4):
                        source = (8 * z + 2 * x + core) * 8 + 4 * h + y
                        x_home, core_home = 2 * h + y // 2, y % 2
                        y_to = other_end(x_home, y, x)
                        away = core ^ (z // 2)
                        section_to = 8 * (z ^ (2 * away)) + 2 * x_home + core_home
                        pairs.append((source, section_to * 8 + 4 * (h ^ away) + y_to))
    return pairs


def position():
    section, rep = lax.axis_index("section"), lax.axis_index("rep")
    return section // 8, section // 2 % 4, section % 2, rep // 4, rep % 4


def swap_core(x):
    return lax.ppermute(x, "section", CORE_PAIRS)


def exchange(x, axis, groups=None):
    return lax.all_to_all(x, axis, 0, 0, tiled=False, axis_index_groups=groups)


def spread(x, count):
    return jnp.broadcast_to(x[None], (count, *x.shape))


def add_up(terms):
    parts = [terms[i].astype(F32) for i in range(terms.shape[0])]
    while len(parts) > 1:
        parts = [parts[i] + parts[i + 1] for i in range(0, len(parts), 2)]
    return parts[0].astype(BF16)


def densify_kernel(scalars_ref, rows_ref, cols_ref, blocks_ref, dense_ref, total):
    total[...] = jnp.zeros_like(total)

    def add_slot(slot, carry):
        total[rows_ref[slot], cols_ref[slot]] += blocks_ref[slot].astype(F32)
        return carry

    lax.fori_loop(0, scalars_ref[0], add_slot, 0)
    for i in range(4):
        for j in range(16):
            tile = total[i, j]
            rows, cols = pl.ds(i * BLOCK, BLOCK), pl.ds(j * BLOCK, BLOCK)
            dense_ref[rows, cols] = tile.astype(BF16)


def densify(scalars, tiles, rows, cols):
    return pl.pallas_call(
        densify_kernel,
        out_shape=jax.ShapeDtypeStruct((512, 2048), BF16),
        in_specs=[SMEM, SMEM, SMEM, VMEM],
        out_specs=VMEM,
        scratch_shapes=[pltpu.VMEM((4, 16, BLOCK, BLOCK), F32)],
        compiler_params=pltpu.CompilerParams(vmem_limit_bytes=20 * 1024 * 1024),
        cost_estimate=pl.CostEstimate(flops=2**22, bytes_accessed=12 * 2**20, transcendentals=0),
    )(scalars, rows, cols, tiles)


def forward_kernel(dense_ref, own_ref, other_ref, out_ref, columns):
    z, _, core, _, _ = position()
    panel = z ^ (2 * core)
    for x in range(4):
        for pair in range(2):
            place = (2 * x + pair) * BLOCK
            own_start = (panel ^ pair) * 512 + x * BLOCK
            other_start = (panel ^ 2 ^ pair) * 512 + x * BLOCK
            columns[pl.ds(pl.multiple_of(own_start, BLOCK), BLOCK), :] = own_ref[
                place : place + BLOCK, :
            ]
            columns[pl.ds(pl.multiple_of(other_start, BLOCK), BLOCK), :] = other_ref[
                place : place + BLOCK, :
            ]
    out_ref[...] = jnp.dot(dense_ref[...], columns[...], preferred_element_type=F32).astype(BF16)


def forward_product(dense, own, other):
    return pl.pallas_call(
        forward_kernel,
        out_shape=jax.ShapeDtypeStruct((512, 256), BF16),
        in_specs=[VMEM, VMEM, VMEM],
        out_specs=VMEM,
        scratch_shapes=[pltpu.VMEM((2048, 256), BF16)],
        compiler_params=pltpu.CompilerParams(vmem_limit_bytes=16 * 1024 * 1024),
    )(dense, own, other)


def prepare_kernel(
    dense_ref,
    degrees_ref,
    features_ref,
    w_self_ref,
    flipped_ref,
    scale_ref,
    chunk_scale_ref,
    base_ref,
):
    for i in range(4):
        for j in range(16):
            rows, cols = pl.ds(i * BLOCK, BLOCK), pl.ds(j * BLOCK, BLOCK)
            flipped_ref[cols, rows] = dense_ref[rows, cols].astype(F32).T.astype(BF16)
    inverse = 1.0 / degrees_ref[...].astype(F32)
    for i in range(4):
        turned = jnp.broadcast_to(inverse[i : i + 1, :], (BLOCK, BLOCK)).T
        scale_ref[i * BLOCK : (i + 1) * BLOCK, :] = turned
    _, _, _, _, y = position()
    chunk_scale = scale_ref[pl.ds(pl.multiple_of(y * BLOCK, BLOCK), BLOCK), :]
    chunk_scale_ref[...] = jnp.concatenate([chunk_scale, chunk_scale], axis=1)
    base_ref[...] = jnp.dot(features_ref[...], w_self_ref[...], preferred_element_type=F32)


def prepare(dense, degrees, features, w_self):
    return pl.pallas_call(
        prepare_kernel,
        out_shape=(
            jax.ShapeDtypeStruct((2048, 512), BF16),
            jax.ShapeDtypeStruct((512, BLOCK), F32),
            jax.ShapeDtypeStruct((BLOCK, 256), F32),
            jax.ShapeDtypeStruct((512, 256), F32),
        ),
        in_specs=[VMEM] * 4,
        out_specs=(VMEM,) * 4,
        compiler_params=pltpu.CompilerParams(vmem_limit_bytes=16 * 1024 * 1024),
        cost_estimate=pl.CostEstimate(flops=2**27, bytes_accessed=5 * 2**20, transcendentals=0),
    )(dense, degrees, features, w_self)


def transposed_product(flipped_ref, panel, down_ref, out_ref):
    for pair in range(2):
        for part in range(2):
            start = pl.multiple_of((panel ^ pair) * 512 + part * 256, 256)
            term = jnp.dot(
                flipped_ref[pl.ds(start, 256), :], down_ref[...], preferred_element_type=F32
            ).astype(out_ref.dtype)
            for x in range(2):
                place = (4 * part + 2 * x + pair) * BLOCK
                out_ref[place : place + BLOCK, :] = term[x * BLOCK : (x + 1) * BLOCK]


def own_kernel(flipped_ref, down_ref, own_ref):
    z, _, core, _, _ = position()
    transposed_product(flipped_ref, 2 * core + z % 2, down_ref, own_ref)


def own_product(flipped, down):
    return pl.pallas_call(
        own_kernel,
        out_shape=jax.ShapeDtypeStruct((1024, 256), F32),
        in_specs=[VMEM, VMEM],
        out_specs=VMEM,
        compiler_params=pltpu.CompilerParams(vmem_limit_bytes=16 * 1024 * 1024),
        cost_estimate=pl.CostEstimate(flops=2**28, bytes_accessed=4 * 2**20, transcendentals=0),
    )(flipped, down)


def middle_kernel(
    mean_ref,
    scale_ref,
    base_ref,
    features_ref,
    cotangent_ref,
    w_neigh_ref,
    flipped_ref,
    preact_ref,
    pre_grad_ref,
    down_ref,
    grad_ref,
    other_ref,
    inputs,
):
    z, _, core, _, y = position()
    first = core == 0
    scale = jnp.concatenate([scale_ref[...], scale_ref[...]], axis=1)
    mean_input = mean_ref[...]
    inputs[:, :256] = features_ref[...]
    inputs[:, 256:] = mean_input
    preact = base_ref[...] + jnp.dot(mean_input, w_neigh_ref[...], preferred_element_type=F32)
    sigmoid_value = jax.nn.sigmoid(preact)
    preact_ref[...] = preact
    slope_value = sigmoid_value * (1.0 + preact * (1.0 - sigmoid_value))
    pre_grad = (cotangent_ref[...].astype(F32) * slope_value).astype(BF16)
    pre_grad_ref[...] = pre_grad
    down_ref[...] = (
        lax.dot_general(pre_grad, w_neigh_ref[...], ROWS_T, preferred_element_type=F32)
        * scale
    ).astype(BF16)
    transposed_product(flipped_ref, (2 * core + z % 2) ^ 2, down_ref, other_ref)
    slice_start = pl.multiple_of(y * BLOCK, BLOCK)
    term = lax.dot_general(
        inputs[:, pl.ds(slice_start, BLOCK)], pre_grad, COLS_T, preferred_element_type=F32
    )
    grad_ref[...] = jnp.where(first, term[:HALF], term[HALF:])
    other_ref[1024:, :] = jnp.where(first, term[HALF:], term[:HALF]).astype(BF16)


def middle(*operands):
    return pl.pallas_call(
        middle_kernel,
        out_shape=(
            jax.ShapeDtypeStruct((512, 256), F32),
            jax.ShapeDtypeStruct((512, 256), BF16),
            jax.ShapeDtypeStruct((512, 256), BF16),
            jax.ShapeDtypeStruct((HALF, 256), F32),
            jax.ShapeDtypeStruct((1088, 256), BF16),
        ),
        in_specs=[VMEM] * 7,
        out_specs=(VMEM,) * 5,
        scratch_shapes=[
            pltpu.VMEM((512, 512), BF16),
        ],
        compiler_params=pltpu.CompilerParams(vmem_limit_bytes=24 * 1024 * 1024),
    )(*operands)


def activate_kernel(preact_ref, pre_grad_ref, w_self_ref, activated_ref, self_part_ref):
    preact = preact_ref[...]
    activated_ref[...] = (preact * jax.nn.sigmoid(preact)).astype(BF16)
    self_part_ref[...] = lax.dot_general(
        pre_grad_ref[...], w_self_ref[...], ROWS_T, preferred_element_type=F32
    )


def activate(preact, pre_grad, w_self):
    return pl.pallas_call(
        activate_kernel,
        out_shape=(
            jax.ShapeDtypeStruct((512, 256), BF16),
            jax.ShapeDtypeStruct((512, 256), F32),
        ),
        in_specs=[VMEM] * 3,
        out_specs=(VMEM,) * 2,
        compiler_params=pltpu.CompilerParams(vmem_limit_bytes=16 * 1024 * 1024),
        cost_estimate=pl.CostEstimate(flops=2**26, bytes_accessed=2**20, transcendentals=2**17),
    )(preact, pre_grad, w_self)


def feature_kernel(results_ref, self_part_ref, feature_ref):
    _, x, core, _, _ = position()
    last = other_end(x, x % 2 * 2 + core, 0)
    for block in range(4):
        rows = slice(block * BLOCK, (block + 1) * BLOCK)
        y = (last + 4 - block) % 4
        feature_ref[rows, :] = self_part_ref[rows, :] + results_ref[y, :BLOCK, :].astype(F32)


def finish_features(results, self_part):
    return pl.pallas_call(
        feature_kernel,
        out_shape=jax.ShapeDtypeStruct((512, 256), F32),
        in_specs=[VMEM] * 2,
        out_specs=VMEM,
        compiler_params=pltpu.CompilerParams(vmem_limit_bytes=16 * 1024 * 1024),
        cost_estimate=pl.CostEstimate(flops=2**27, bytes_accessed=2**21, transcendentals=0),
    )(results, self_part)


def grad_kernel(own_ref, other_ref, self_ref, neigh_ref):
    first = position()[2] == 0
    for y in range(4):
        own, other = own_ref[y].astype(F32), other_ref[y].astype(F32)
        target = self_ref if y < 2 else neigh_ref
        start = y % 2 * BLOCK
        target[start : start + HALF, :] = jnp.where(first, own, other)
        target[start + HALF : start + BLOCK, :] = jnp.where(first, other, own)


def finish_grads(own, other):
    return pl.pallas_call(
        grad_kernel,
        out_shape=(
            jax.ShapeDtypeStruct((256, 256), F32),
            jax.ShapeDtypeStruct((256, 256), F32),
        ),
        in_specs=[VMEM] * 2,
        out_specs=(VMEM,) * 2,
        compiler_params=pltpu.CompilerParams(vmem_limit_bytes=16 * 1024 * 1024),
    )(own, other)


def body(
    features, cotangent, degrees, blocks, block_rows, block_cols, block_count, w_self, w_neigh
):
    z, x, core, h, y = position()
    y_column = x % 2 * 2 + core
    scalars = jnp.stack([block_count[0, 0], core.astype(jnp.int32)])
    with jax.named_scope("spread_features"):
        place = other_end(x, y_column, y)
        block = lax.dynamic_index_in_dim(
            features.reshape(4, BLOCK, 256), place, 0, keepdims=False
        )
        block = lax.ppermute(block, ("section", "rep"), out_pairs())
        block, scalars = lax.optimization_barrier((block, scalars))
    with jax.named_scope("gather_features"):
        pair = jnp.stack([block, lax.ppermute(block, "section", NEXT_Z)])
        own_columns = exchange(spread(pair, 4), "section", SAME_ZC).reshape(1024, 256)
        own_columns, row_slots = lax.optimization_barrier((own_columns, block_rows[0, 0]))
        other_columns = swap_core(own_columns)
    dense = densify(scalars, blocks[0, 0], row_slots, block_cols[0, 0])
    partial = forward_product(dense, own_columns, other_columns)
    with jax.named_scope("sum_over_y"):
        partial = add_up(exchange(partial.reshape(4, BLOCK, 256), "rep", SAME_H))
    with jax.named_scope("sum_over_h"):
        partial, degree_rows = lax.optimization_barrier((partial, degrees.reshape(4, BLOCK)))
        arrived = lax.ppermute(partial, "rep", HALF_PAIRS)
        flipped, scale, chunk_scale, base = prepare(dense, degree_rows, features, w_self)
        summed = partial.astype(F32) + arrived.astype(F32)
        mean_chunk = (summed * chunk_scale).astype(BF16)
    with jax.named_scope("gather_over_y"):
        mean_chunk, flipped = lax.optimization_barrier((mean_chunk, flipped))
        mean_input = exchange(spread(mean_chunk, 4), "rep", SAME_H)
    preact, pre_grad, down, own_grad, other = middle(
        mean_input.reshape(512, 256), scale, base, features, cotangent, w_neigh, flipped
    )
    with jax.named_scope("pair_sum"):
        arrived = swap_core(other)
        own = own_product(flipped, down)
        main = (own + arrived[:1024].astype(F32)).astype(BF16).reshape(4, 256, 256)
        grad_part = (own_grad + arrived[1024:].astype(F32)).astype(BF16)
        send = jnp.concatenate([main, spread(grad_part, 4)], axis=1)
    with jax.named_scope("sum_over_section"):
        total = add_up(exchange(send, "section", SAME_ZC))
        arrived = lax.ppermute(total[BLOCK:], "section", NEXT_Z)
        kept = jnp.concatenate([total[:BLOCK], total[256:]])
        total = (kept.astype(F32) + arrived.astype(F32)).astype(BF16)
        arrived = lax.ppermute(total, "section", Z_PAIRS)
        total = (total.astype(F32) + arrived.astype(F32)).astype(BF16)
    with jax.named_scope("return_panels"):
        block = lax.ppermute(total[:BLOCK], ("section", "rep"), back_pairs())
        activated, self_part = activate(preact, pre_grad, w_self)
        block, activated, self_part = lax.optimization_barrier((block, activated, self_part))
    with jax.named_scope("gather_results"):
        last = jnp.concatenate([block, total[BLOCK:]], axis=0)
        results = exchange(spread(last, 4), "rep", SAME_H)
        own_rows = results[:, BLOCK:]
        other_rows = swap_core(own_rows)
    feature_grad = finish_features(results, self_part)
    grad_self, grad_neigh = finish_grads(own_rows, other_rows)
    return (activated, feature_grad, grad_self, grad_neigh)


def solution(mesh):
    return jax.shard_map(
        body,
        mesh=mesh,
        in_specs=(
            P("section", None),
            P("section", None),
            P("section"),
            P("section", "rep", None, None, None),
            P("section", "rep", None),
            P("section", "rep", None),
            P("section", "rep"),
            P(),
            P(),
        ),
        out_specs=(P("section", None), P("section", None), P(), P()),
        check_vma=False,
    )
```

```python
import jax
import jax.numpy as jnp
from jax import lax
from jax.experimental import pallas as pl
from jax.experimental.pallas import tpu as pltpu
from jax.sharding import PartitionSpec as P

BLOCK = 128
HALF = 64
F32 = jnp.float32
BF16 = jnp.bfloat16
ROWS_T = (((1,), (1,)), ((), ()))
COLS_T = (((0,), (0,)), ((), ()))
SMEM = pl.BlockSpec(memory_space=pltpu.SMEM)
VMEM = pl.BlockSpec(memory_space=pltpu.VMEM)

CORE_PAIRS = [(s, s ^ 1) for s in range(32)]
HALF_PAIRS = [(r, r ^ 4) for r in range(8)]
NEXT_Z = [(s, s ^ 8) for s in range(32)]
Z_PAIRS = [(s, s ^ 16) for s in range(32)]
SAME_ZC = [[8 * z + 2 * x + core for x in range(4)] for z in range(4) for core in range(2)]
SAME_H = [[4 * h + i for i in range(4)] for h in range(2)]


def other_end(x_home, y_column, place):
    return (x_home + y_column + 2 - place) % 4


def out_pairs():
    pairs = []
    for z in range(4):
        for x in range(4):
            for core in range(2):
                h, y_column = x // 2, (x % 2) * 2 + core
                for y in range(4):
                    for core_to in range(2):
                        source = (8 * z + 2 * x + core) * 8 + 4 * (h ^ core_to) + y
                        x_to = other_end(x, y_column, y)
                        section_to = 8 * (z ^ (2 * core_to)) + 2 * x_to + core_to
                        pairs.append((source, section_to * 8 + 4 * h + y_column))
    return pairs


def back_pairs():
    pairs = []
    for z in range(4):
        for x in range(4):
            for core in range(2):
                for h in range(2):
                    for y in range(4):
                        source = (8 * z + 2 * x + core) * 8 + 4 * h + y
                        x_home, core_home = 2 * h + y // 2, y % 2
                        y_to = other_end(x_home, y, x)
                        away = core ^ (z // 2)
                        section_to = 8 * (z ^ (2 * away)) + 2 * x_home + core_home
                        pairs.append((source, section_to * 8 + 4 * (h ^ away) + y_to))
    return pairs


def position():
    section, rep = lax.axis_index("section"), lax.axis_index("rep")
    return section // 8, section // 2 % 4, section % 2, rep // 4, rep % 4


def swap_core(x):
    return lax.ppermute(x, "section", CORE_PAIRS)


def exchange(x, axis, groups=None):
    return lax.all_to_all(x, axis, 0, 0, tiled=False, axis_index_groups=groups)


def spread(x, count):
    return jnp.broadcast_to(x[None], (count, *x.shape))


def add_up(terms):
    parts = [terms[i].astype(F32) for i in range(terms.shape[0])]
    while len(parts) > 1:
        parts = [parts[i] + parts[i + 1] for i in range(0, len(parts), 2)]
    return parts[0].astype(BF16)


def densify_kernel(scalars_ref, rows_ref, cols_ref, blocks_ref, dense_ref, total):
    total[...] = jnp.zeros_like(total)

    def add_slot(slot, carry):
        total[rows_ref[slot], cols_ref[slot]] += blocks_ref[slot].astype(F32)
        return carry

    lax.fori_loop(0, scalars_ref[0], add_slot, 0)
    for i in range(4):
        for j in range(16):
            tile = total[i, j]
            rows, cols = pl.ds(i * BLOCK, BLOCK), pl.ds(j * BLOCK, BLOCK)
            dense_ref[rows, cols] = tile.astype(BF16)


def densify(scalars, tiles, rows, cols):
    return pl.pallas_call(
        densify_kernel,
        out_shape=jax.ShapeDtypeStruct((512, 2048), BF16),
        in_specs=[SMEM, SMEM, SMEM, VMEM],
        out_specs=VMEM,
        scratch_shapes=[pltpu.VMEM((4, 16, BLOCK, BLOCK), F32)],
        compiler_params=pltpu.CompilerParams(vmem_limit_bytes=20 * 1024 * 1024),
        cost_estimate=pl.CostEstimate(flops=2**22, bytes_accessed=12 * 2**20, transcendentals=0),
    )(scalars, rows, cols, tiles)


def forward_kernel(dense_ref, own_ref, other_ref, out_ref, columns):
    z, _, core, _, _ = position()
    panel = z ^ (2 * core)
    for x in range(4):
        for pair in range(2):
            place = (2 * x + pair) * BLOCK
            own_start = (panel ^ pair) * 512 + x * BLOCK
            other_start = (panel ^ 2 ^ pair) * 512 + x * BLOCK
            columns[pl.ds(pl.multiple_of(own_start, BLOCK), BLOCK), :] = own_ref[
                place : place + BLOCK, :
            ]
            columns[pl.ds(pl.multiple_of(other_start, BLOCK), BLOCK), :] = other_ref[
                place : place + BLOCK, :
            ]
    out_ref[...] = jnp.dot(dense_ref[...], columns[...], preferred_element_type=F32).astype(BF16)


def forward_product(dense, own, other):
    return pl.pallas_call(
        forward_kernel,
        out_shape=jax.ShapeDtypeStruct((512, 256), BF16),
        in_specs=[VMEM, VMEM, VMEM],
        out_specs=VMEM,
        scratch_shapes=[pltpu.VMEM((2048, 256), BF16)],
        compiler_params=pltpu.CompilerParams(vmem_limit_bytes=16 * 1024 * 1024),
    )(dense, own, other)


def prepare_kernel(
    dense_ref,
    degrees_ref,
    features_ref,
    w_self_ref,
    flipped_ref,
    scale_ref,
    chunk_scale_ref,
    base_ref,
):
    for i in range(4):
        for j in range(16):
            rows, cols = pl.ds(i * BLOCK, BLOCK), pl.ds(j * BLOCK, BLOCK)
            flipped_ref[cols, rows] = dense_ref[rows, cols].astype(F32).T.astype(BF16)
    inverse = 1.0 / degrees_ref[...].astype(F32)
    for i in range(4):
        turned = jnp.broadcast_to(inverse[i : i + 1, :], (BLOCK, BLOCK)).T
        scale_ref[i * BLOCK : (i + 1) * BLOCK, :] = turned
    _, _, _, _, y = position()
    chunk_scale = scale_ref[pl.ds(pl.multiple_of(y * BLOCK, BLOCK), BLOCK), :]
    chunk_scale_ref[...] = jnp.concatenate([chunk_scale, chunk_scale], axis=1)
    base_ref[...] = jnp.dot(features_ref[...], w_self_ref[...], preferred_element_type=F32)


def prepare(dense, degrees, features, w_self):
    return pl.pallas_call(
        prepare_kernel,
        out_shape=(
            jax.ShapeDtypeStruct((2048, 512), BF16),
            jax.ShapeDtypeStruct((512, BLOCK), F32),
            jax.ShapeDtypeStruct((BLOCK, 256), F32),
            jax.ShapeDtypeStruct((512, 256), F32),
        ),
        in_specs=[VMEM] * 4,
        out_specs=(VMEM,) * 4,
        compiler_params=pltpu.CompilerParams(vmem_limit_bytes=16 * 1024 * 1024),
        cost_estimate=pl.CostEstimate(flops=2**27, bytes_accessed=5 * 2**20, transcendentals=0),
    )(dense, degrees, features, w_self)


def transposed_product(flipped_ref, panel, down_ref, out_ref):
    for pair in range(2):
        for part in range(2):
            start = pl.multiple_of((panel ^ pair) * 512 + part * 256, 256)
            term = jnp.dot(
                flipped_ref[pl.ds(start, 256), :], down_ref[...], preferred_element_type=F32
            ).astype(out_ref.dtype)
            for x in range(2):
                place = (4 * part + 2 * x + pair) * BLOCK
                out_ref[place : place + BLOCK, :] = term[x * BLOCK : (x + 1) * BLOCK]


def own_kernel(flipped_ref, down_ref, own_ref):
    z, _, core, _, _ = position()
    transposed_product(flipped_ref, 2 * core + z % 2, down_ref, own_ref)


def own_product(flipped, down):
    return pl.pallas_call(
        own_kernel,
        out_shape=jax.ShapeDtypeStruct((1024, 256), F32),
        in_specs=[VMEM, VMEM],
        out_specs=VMEM,
        compiler_params=pltpu.CompilerParams(vmem_limit_bytes=16 * 1024 * 1024),
        cost_estimate=pl.CostEstimate(flops=2**28, bytes_accessed=4 * 2**20, transcendentals=0),
    )(flipped, down)


def middle_kernel(
    mean_ref,
    scale_ref,
    base_ref,
    features_ref,
    cotangent_ref,
    w_neigh_ref,
    flipped_ref,
    preact_ref,
    pre_grad_ref,
    down_ref,
    grad_ref,
    other_ref,
    inputs,
):
    z, _, core, _, y = position()
    first = core == 0
    scale = jnp.concatenate([scale_ref[...], scale_ref[...]], axis=1)
    mean_input = mean_ref[...]
    inputs[:, :256] = features_ref[...]
    inputs[:, 256:] = mean_input
    preact = base_ref[...] + jnp.dot(mean_input, w_neigh_ref[...], preferred_element_type=F32)
    sigmoid_value = jax.nn.sigmoid(preact)
    preact_ref[...] = preact
    slope_value = sigmoid_value * (1.0 + preact * (1.0 - sigmoid_value))
    pre_grad = (cotangent_ref[...].astype(F32) * slope_value).astype(BF16)
    pre_grad_ref[...] = pre_grad
    down_ref[...] = (
        lax.dot_general(pre_grad, w_neigh_ref[...], ROWS_T, preferred_element_type=F32)
        * scale
    ).astype(BF16)
    transposed_product(flipped_ref, (2 * core + z % 2) ^ 2, down_ref, other_ref)
    slice_start = pl.multiple_of(y * BLOCK, BLOCK)
    term = lax.dot_general(
        inputs[:, pl.ds(slice_start, BLOCK)], pre_grad, COLS_T, preferred_element_type=F32
    )
    grad_ref[...] = jnp.where(first, term[:HALF], term[HALF:])
    other_ref[1024:, :] = jnp.where(first, term[HALF:], term[:HALF]).astype(BF16)


def middle(*operands):
    return pl.pallas_call(
        middle_kernel,
        out_shape=(
            jax.ShapeDtypeStruct((512, 256), F32),
            jax.ShapeDtypeStruct((512, 256), BF16),
            jax.ShapeDtypeStruct((512, 256), BF16),
            jax.ShapeDtypeStruct((HALF, 256), F32),
            jax.ShapeDtypeStruct((1088, 256), BF16),
        ),
        in_specs=[VMEM] * 7,
        out_specs=(VMEM,) * 5,
        scratch_shapes=[
            pltpu.VMEM((512, 512), BF16),
        ],
        compiler_params=pltpu.CompilerParams(vmem_limit_bytes=24 * 1024 * 1024),
    )(*operands)


def activate_kernel(preact_ref, pre_grad_ref, w_self_ref, activated_ref, self_part_ref):
    preact = preact_ref[...]
    activated_ref[...] = (preact * jax.nn.sigmoid(preact)).astype(BF16)
    self_part_ref[...] = lax.dot_general(
        pre_grad_ref[...], w_self_ref[...], ROWS_T, preferred_element_type=F32
    )


def activate(preact, pre_grad, w_self):
    return pl.pallas_call(
        activate_kernel,
        out_shape=(
            jax.ShapeDtypeStruct((512, 256), BF16),
            jax.ShapeDtypeStruct((512, 256), F32),
        ),
        in_specs=[VMEM] * 3,
        out_specs=(VMEM,) * 2,
        compiler_params=pltpu.CompilerParams(vmem_limit_bytes=16 * 1024 * 1024),
        cost_estimate=pl.CostEstimate(flops=2**26, bytes_accessed=2**20, transcendentals=2**17),
    )(preact, pre_grad, w_self)


def feature_kernel(results_ref, self_part_ref, feature_ref):
    _, x, core, _, _ = position()
    last = other_end(x, x % 2 * 2 + core, 0)
    for block in range(4):
        rows = slice(block * BLOCK, (block + 1) * BLOCK)
        y = (last + 4 - block) % 4
        feature_ref[rows, :] = self_part_ref[rows, :] + results_ref[y, :BLOCK, :].astype(F32)


def finish_features(results, self_part):
    return pl.pallas_call(
        feature_kernel,
        out_shape=jax.ShapeDtypeStruct((512, 256), F32),
        in_specs=[VMEM] * 2,
        out_specs=VMEM,
        compiler_params=pltpu.CompilerParams(vmem_limit_bytes=16 * 1024 * 1024),
        cost_estimate=pl.CostEstimate(flops=2**27, bytes_accessed=2**21, transcendentals=0),
    )(results, self_part)


def finish_grads(own, other, first):
    top, bottom = jnp.where(first, own, other), jnp.where(first, other, own)
    rows = jnp.concatenate([top, bottom], axis=1).astype(F32)
    return rows[:2].reshape(256, 256), rows[2:].reshape(256, 256)


def body(
    features, cotangent, degrees, blocks, block_rows, block_cols, block_count, w_self, w_neigh
):
    z, x, core, h, y = position()
    y_column = x % 2 * 2 + core
    scalars = jnp.stack([block_count[0, 0], core.astype(jnp.int32)])
    with jax.named_scope("spread_features"):
        place = other_end(x, y_column, y)
        block = lax.dynamic_index_in_dim(
            features.reshape(4, BLOCK, 256), place, 0, keepdims=False
        )
        block = lax.ppermute(block, ("section", "rep"), out_pairs())
        block, scalars = lax.optimization_barrier((block, scalars))
    with jax.named_scope("gather_features"):
        pair = jnp.stack([block, lax.ppermute(block, "section", NEXT_Z)])
        own_columns = exchange(spread(pair, 4), "section", SAME_ZC).reshape(1024, 256)
        own_columns, row_slots = lax.optimization_barrier((own_columns, block_rows[0, 0]))
        other_columns = swap_core(own_columns)
    dense = densify(scalars, blocks[0, 0], row_slots, block_cols[0, 0])
    partial = forward_product(dense, own_columns, other_columns)
    with jax.named_scope("sum_over_y"):
        partial = add_up(exchange(partial.reshape(4, BLOCK, 256), "rep", SAME_H))
    with jax.named_scope("sum_over_h"):
        partial, degree_rows = lax.optimization_barrier((partial, degrees.reshape(4, BLOCK)))
        arrived = lax.ppermute(partial, "rep", HALF_PAIRS)
        flipped, scale, chunk_scale, base = prepare(dense, degree_rows, features, w_self)
        summed = partial.astype(F32) + arrived.astype(F32)
        mean_chunk = (summed * chunk_scale).astype(BF16)
    with jax.named_scope("gather_over_y"):
        mean_chunk, flipped = lax.optimization_barrier((mean_chunk, flipped))
        mean_input = exchange(spread(mean_chunk, 4), "rep", SAME_H)
    preact, pre_grad, down, own_grad, other = middle(
        mean_input.reshape(512, 256), scale, base, features, cotangent, w_neigh, flipped
    )
    with jax.named_scope("pair_sum"):
        arrived = swap_core(other)
        own = own_product(flipped, down)
        main = (own + arrived[:1024].astype(F32)).astype(BF16).reshape(4, 256, 256)
        grad_part = (own_grad + arrived[1024:].astype(F32)).astype(BF16)
        send = jnp.concatenate([main, spread(grad_part, 4)], axis=1)
    with jax.named_scope("sum_over_section"):
        total = add_up(exchange(send, "section", SAME_ZC))
        arrived = lax.ppermute(total[BLOCK:], "section", NEXT_Z)
        kept = jnp.concatenate([total[:BLOCK], total[256:]])
        total = (kept.astype(F32) + arrived.astype(F32)).astype(BF16)
        arrived = lax.ppermute(total, "section", Z_PAIRS)
        total = (total.astype(F32) + arrived.astype(F32)).astype(BF16)
    with jax.named_scope("return_panels"):
        block = lax.ppermute(total[:BLOCK], ("section", "rep"), back_pairs())
        activated, self_part = activate(preact, pre_grad, w_self)
        block, activated, self_part = lax.optimization_barrier((block, activated, self_part))
    with jax.named_scope("gather_results"):
        last = jnp.concatenate([block, total[BLOCK:]], axis=0)
        results = exchange(spread(last, 4), "rep", SAME_H)
        own_rows = results[:, BLOCK:]
        other_rows = swap_core(own_rows)
    feature_grad = finish_features(results, self_part)
    grad_self, grad_neigh = finish_grads(own_rows, other_rows, core == 0)
    return (activated, feature_grad, grad_self, grad_neigh)


def solution(mesh):
    return jax.shard_map(
        body,
        mesh=mesh,
        in_specs=(
            P("section", None),
            P("section", None),
            P("section"),
            P("section", "rep", None, None, None),
            P("section", "rep", None),
            P("section", "rep", None),
            P("section", "rep"),
            P(),
            P(),
        ),
        out_specs=(P("section", None), P("section", None), P(), P()),
        check_vma=False,
    )
```
